256 devices in a mesh: wide: 32 (over x, z), narrow: 8 (over y, core).
Axes of the slice: x: 4, y: 4, z: 8, core: 2. Of those that a mesh axis runs over, the one named last changes fastest.
Arguments:
- particle_populations: float32 [64, 2048, 128], P('narrow', 'wide'), may hold values from 0.5 to 2
- kinetic_coefficient_list: float32 [128, 64], replicated, may hold values from -0.75 to 0.75
- stoichiometry_table: float32 [64, 128], replicated, may hold values from -0.5 to 0.5
- sampled_event_draws: int32 [2, 128, 2048, 128], P(None, None, ('wide', 'narrow')), may hold values from 0 to 7
- spreading_rates: float32 [64], P('narrow'), may hold values from 0.02 to 0.12
- adjacency_lists: int32 [2048, 4], P('wide'), may hold values from 0 to 2047, as said below
- adjacent_hop_tallies: int32 [2, 2048, 4], P(None, 'wide'), may hold values from 0 to 3
- current_per_molecule: float32 [64], P('narrow'), may hold values from -1 to 1
- target_boundary_node: int32 [2048, 128], P('wide'), may hold values from 0 to 8191
- membrane_storage_factor: float32 [256, 1024], P('wide', 'narrow'), may hold values from 0.05 to 0.5
- prior_voltage: float32 [256, 1024], P('wide', 'narrow'), may hold values from -6 to 6
Outputs:
- amounts_out: float32 [64, 2048, 128], P('narrow', 'wide')
- potential: float32 [256, 1024], P('wide', 'narrow')
The draws below stay inside these ranges and needn't reach their ends.
Inputs may be any that keep to these rules, and one draw needn't show every extreme that they name: `adjacency_lists`: each entry names a block at most 64 blocks away from its own; a block may name itself, which adds nothing.
All inputs are finite; a program needn't handle non-finite values.
Results may differ from the reference program's by a relative error of at most 0.0003.
Values sent between devices are 32-bit elements; how exact they have to be, the bound alone decides.
A program may use at most 64 MiB of HBM per device.

```python
import math
import jax
import jax.numpy as jnp
import numpy as np
from jax import lax

SP = 64
CHANNEL_NUMBER = 128
CELLS_PER_GROUP = 128
NBR = 4
INTERVAL_NUMBER = 2
ITERS = 3
NB_DEV = 64
VX_DEV = 8
GROUP_NUMBER = 2048
VX = 256
VY = 1024


def draw_adjacency_lists(key, part):
    key = jax.random.fold_in(key, 11)
    first_key, second_key, third_key = jax.random.split(key, 3)
    blocks = jnp.arange(GROUP_NUMBER, dtype=jnp.int32)
    back_step = jax.random.randint(first_key, (GROUP_NUMBER,), 1, NB_DEV + 1).astype(jnp.int32)
    back_step = jnp.where(blocks % NB_DEV == NB_DEV - 1, NB_DEV, back_step)
    forward_step = jax.random.randint(second_key, (GROUP_NUMBER,), 1, NB_DEV + 1).astype(jnp.int32)
    forward_step = jnp.where(blocks % NB_DEV == 0, NB_DEV, forward_step)
    nearby = jax.random.randint(third_key, (GROUP_NUMBER, NBR - 2), -NB_DEV, NB_DEV + 1).astype(jnp.int32)
    candidate = jnp.concatenate([(blocks - back_step)[:, None], (blocks + forward_step)[:, None], blocks[:, None] + nearby], axis=1)
    inside = (candidate >= 0) & (candidate < GROUP_NUMBER)
    return jnp.where(inside, candidate, blocks[:, None]).astype(jnp.int32)


def with_ends(entries, key, low, high):
    shape = entries.shape
    spot = [jax.random.randint(jax.random.fold_in(key, axis), (), 0, shape[axis]) for axis in range(len(shape))]
    entries = entries.at[tuple(spot)].set(low)
    longest = shape.index(max(shape))
    spot[longest] = (spot[longest] + 1) % shape[longest]
    return entries.at[tuple(spot)].set(high)


def shard_levels(key, shape, cuts, low, high):
    gain = 1.0
    for axis_at, shards_of in cuts:
        draws = jax.random.uniform(jax.random.fold_in(jax.random.fold_in(key, 6), axis_at), (shards_of,), jnp.float32, low / len(cuts), high / len(cuts))
        gain = gain * jnp.repeat(jnp.exp(draws), shape[axis_at] // shards_of).reshape((-1,) + (1,) * (len(shape) - 1 - axis_at))
    return gain


def cumulative_ranks(count, skew):
    weights = [(1 << 20) // math.isqrt(grade ** skew) + 1 for grade in range(1, count + 1)]
    deviation = 1 + sum(weights) // (1 << 30)
    return np.cumsum(np.array([max(1, weight // deviation) for weight in weights]))


def skewed_ids(rng, dims, count, skew):
    table = cumulative_ranks(count, skew)
    pick = jax.random.randint(jax.random.fold_in(rng, 1), dims, 0, int(table[count - 1]))
    rank = jnp.searchsorted(jnp.asarray(table, jnp.int32), pick, side="right")
    return jax.random.permutation(jax.random.fold_in(rng, 2), count)[rank].astype(jnp.int32)


def scatter_about(stream_key, shape, spread, reach, shards=(), kind=jnp.bfloat16):
    result = jax.random.normal(stream_key, shape, jnp.float32) * spread
    if len(shards) > 0:
        result = shard_levels(stream_key, shape, shards, -0.22, 0.18) * result
    return jnp.clip(result, min=-reach, max=reach).astype(kind)


def setup_inputs(seed: int = 0) -> dict:
    key_list = jax.random.split(jax.random.key(seed), 12)
    return {
        "particle_populations": jnp.clip(0.5 + 1.5 * jax.random.uniform(key_list[0], (SP, GROUP_NUMBER, CELLS_PER_GROUP), jnp.float32) ** shard_levels(key_list[0], (SP, GROUP_NUMBER, CELLS_PER_GROUP), ((0, 8), (1, 32)), -0.2, 0.2), 0.5, 2.0),
        "kinetic_coefficient_list": scatter_about(key_list[1], (CHANNEL_NUMBER, SP), SP ** -0.5, 0.75, (), jnp.float32),
        "stoichiometry_table": scatter_about(key_list[2], (SP, CHANNEL_NUMBER), CHANNEL_NUMBER ** -0.5, 0.5, (), jnp.float32),
        "sampled_event_draws": with_ends(jax.random.randint(key_list[3], (INTERVAL_NUMBER, CHANNEL_NUMBER, GROUP_NUMBER, CELLS_PER_GROUP), 0, 8), jax.random.fold_in(key_list[3], 1), 0, 7).astype(jnp.int32),
        "spreading_rates": jnp.clip(jnp.exp(math.log(0.12) - 1.7917595 * jax.random.uniform(key_list[4], (SP,), jnp.float32) ** shard_levels(key_list[4], (SP,), ((0, 8),), -0.2, 0.2)), 0.02, 0.12),
        "adjacency_lists": draw_adjacency_lists(jax.random.fold_in(key_list[11], 71), 0),
        "adjacent_hop_tallies": with_ends(jax.random.randint(key_list[6], (INTERVAL_NUMBER, GROUP_NUMBER, NBR), 0, 4), jax.random.fold_in(key_list[6], 1), 0, 3).astype(jnp.int32),
        "current_per_molecule": scatter_about(key_list[7], (SP,), 0.125, 1.0, ((0, 8),), jnp.float32),
        "target_boundary_node": with_ends(skewed_ids(key_list[8], (GROUP_NUMBER, CELLS_PER_GROUP), VX_DEV * VY, 1), jax.random.fold_in(key_list[8], 3), 0, (VX_DEV * VY) - 1).astype(jnp.int32),
        "membrane_storage_factor": jnp.clip(jnp.exp(math.log(0.5) - 2.3025851 * jax.random.uniform(key_list[9], (VX, VY), jnp.float32) ** shard_levels(key_list[9], (VX, VY), ((0, 32), (1, 8)), -0.2, 0.2)), 0.05, 0.5),
        "prior_voltage": scatter_about(key_list[10], (VX, VY), 1.0, 6.0, ((0, 32), (1, 8)), jnp.float32),
    }


def chemistry_progress(particle_populations, kinetic_coefficient_list, stoichiometry_table, sampled_event_draws):
    intensity_of_event = jnp.einsum("cl,lug->cug", kinetic_coefficient_list, particle_populations, precision=lax.Precision.HIGHEST)
    realized_event_tally = intensity_of_event * (sampled_event_draws.astype(jnp.float32) * (1.0 / 3.5))
    stoichiometric_shift = jnp.einsum("xk,kdl->xdl", stoichiometry_table, realized_event_tally, precision=lax.Precision.HIGHEST)
    return particle_populations + 0.25 * stoichiometric_shift


def diffuse(particle_populations, spreading_rates, adjacency_lists, adjacent_hop_tallies):
    weights = adjacent_hop_tallies.astype(jnp.float32) * 0.5
    flux_sum = jnp.zeros_like(particle_populations)
    for slot_index in range(adjacency_lists.shape[1]):
        picked = jnp.take(particle_populations, adjacency_lists[:, slot_index], axis=1)
        flux_sum = flux_sum + weights[:, slot_index][None, :, None] * (picked - particle_populations)
    return particle_populations + spreading_rates[:, None, None] * flux_sum


def membrane(field, membrane_storage_factor):
    padded = jnp.pad(field, 1)
    beside_all = padded[2:, 1:-1] + padded[:-2, 1:-1] + padded[1:-1, 2:] + padded[1:-1, :-2]
    return (4.0 + membrane_storage_factor) * field - beside_all


def reference(particle_populations, kinetic_coefficient_list, stoichiometry_table, sampled_event_draws, spreading_rates, adjacency_lists, adjacent_hop_tallies, current_per_molecule, target_boundary_node, membrane_storage_factor, prior_voltage):
    for poisson_interval_progress in range(INTERVAL_NUMBER):
        particle_populations = chemistry_progress(particle_populations, kinetic_coefficient_list, stoichiometry_table, sampled_event_draws[poisson_interval_progress])
        particle_populations = diffuse(particle_populations, spreading_rates, adjacency_lists, adjacent_hop_tallies[poisson_interval_progress])
    current = jnp.einsum("s,sbt->bt", current_per_molecule, particle_populations, precision=lax.Precision.HIGHEST)
    owner = (jnp.arange(GROUP_NUMBER, dtype=jnp.int32) // NB_DEV) * (VX_DEV * VY)
    flat_index = (target_boundary_node + owner[:, None]).astype(jnp.int32)
    source = jax.ops.segment_sum(current.reshape(-1), flat_index.reshape(-1), num_segments=VX * VY).reshape(VX, VY)
    right_side = membrane_storage_factor * prior_voltage + source
    potential = jnp.zeros_like(right_side)
    residual = right_side
    direction = right_side
    norm_now = jnp.sum(residual * residual)
    for iteration in range(ITERS):
        applied = membrane(direction, membrane_storage_factor)
        step_size = norm_now / jnp.sum(direction * applied)
        potential = potential + step_size * direction
        residual = residual - step_size * applied
        norm_next = jnp.sum(residual * residual)
        direction = residual + (norm_next / norm_now) * direction
        norm_now = norm_next
    return particle_populations, potential
```

```python
import functools

import jax
import jax.numpy as jnp
from jax import lax
from jax.experimental import pallas as pl
from jax.experimental.pallas import tpu as pltpu
from jax.sharding import PartitionSpec as P

MESH = pl.DeviceIdType.MESH
F32 = jnp.float32
BF16 = jnp.bfloat16

PARTNERS = ((1, 0), (3, 0), (1, 1), (3, 1), (2, 0), (2, 1), (0, 1))
DIRECT = ((0, 1), (1, 0), (3, 0), (1, 1), (3, 1))
SHIFT = 4.0


def split(x):
    high = x.astype(BF16)
    return high, (x - high.astype(F32)).astype(BF16)


def dot(a, b):
    return jnp.dot(a, b, preferred_element_type=F32)


def dot_nt(a, b):
    return lax.dot_general(a, b, (((1,), (1,)), ((), ())), preferred_element_type=F32)


def iota(shape, dim):
    return lax.broadcasted_iota(jnp.int32, shape, dim)


def inner(p, q, moments):
    total = None
    for i, pi in enumerate(p):
        for j, qj in enumerate(q):
            term = pi * qj * moments[i + j]
            total = term if total is None else total + term
    return total


def krylov_coefficients(moments):
    one = jnp.ones_like(moments[0])
    direction, residual = [one], [one]
    x = [jnp.zeros_like(one)] * 3
    norm = moments[0]
    for iteration in range(3):
        size = len(direction)
        applied = [SHIFT * d for d in direction] + [jnp.zeros_like(one)]
        for i in range(size):
            applied[i + 1] = applied[i + 1] + direction[i]
        step = norm / inner(direction, applied, moments)
        x = [x[i] + step * direction[i] if i < size else x[i] for i in range(3)]
        if iteration == 2:
            return x
        residual = [
            (residual[i] if i < len(residual) else 0.0) - step * applied[i] for i in range(size + 1)
        ]
        fresh = inner(residual, residual, moments)
        ratio = fresh / norm
        norm = fresh
        direction = [
            residual[i] + ratio * direction[i] if i < size else residual[i] for i in range(size + 1)
        ]


def kernel(
    zs, xs,
    pops, kct, sto, draws, rates, adjt, talt, coef, tgt, msf, prior,
    out_pops, out_pot,
    gath, react, halo, diff, draws_v, kct_v, sto_v, adj_v, tal_v, tgt_v, msf_v, pri_v,
    rate_s, coef_s, ep, msfh, kmat, smat, wmat, lot, him, uv, vh, fields, mz, mx,
    loc, dloc, sa, ra, sh, r2, rh, se, re, su, ru, sg, rg, so,
):
    w, n = lax.axis_index("wide"), lax.axis_index("narrow")
    wides = zs * xs
    left, right = lax.rem(w + wides - 1, wides), lax.rem(w + 1, wides)
    y, core = n // 2, lax.rem(n, 2)
    x, z = w // zs, lax.rem(w, zs)

    def peer(rel):
        return lax.rem(y + rel[0], 4) * 2 + lax.rem(core + rel[1], 2)

    def source(rel):
        return peer(((4 - rel[0]) % 4, rel[1]))

    def eight(i):
        return pl.ds(pl.multiple_of(i * 8, 8), 8)

    def send(src, dst, s, r, to):
        pltpu.make_async_remote_copy(
            src_ref=src, dst_ref=dst, send_sem=s, recv_sem=r, device_id=to, device_id_type=MESH
        ).start()

    def wait(ref, sem):
        pltpu.make_async_copy(ref, ref, sem).wait()

    z_line = [x * zs + lax.rem(z + k, zs) for k in range(1, zs)]
    x_line = [lax.rem(x + k, xs) * zs + z for k in range(1, xs)]

    barrier = pltpu.get_barrier_semaphore()
    greet = [(w, peer(rel)) for rel in PARTNERS]
    for side in (left, right):
        greet += [(side, n)] + [(side, peer(rel)) for rel in PARTNERS]
    greet += [(v, n) for v in z_line + x_line]
    for to in greet:
        pl.semaphore_signal(barrier, inc=1, device_id=to, device_id_type=MESH)

    small = [
        (coef, coef_s), (rates, rate_s), (msf, msf_v), (prior, pri_v), (kct, kct_v), (sto, sto_v),
        (adjt, adj_v), (talt, tal_v), (tgt, tgt_v), (pops.at[:, eight(n), :], gath.at[0, eight(n)]),
    ]
    small = [pltpu.make_async_copy(s, d, loc.at[i]) for i, (s, d) in enumerate(small)]
    for copy in small:
        copy.start()
    for k in range(2):
        for b in range(8):
            pltpu.make_async_copy(draws.at[k, :, b, :], draws_v.at[k, b], dloc.at[k]).start()
    pl.semaphore_wait(barrier, len(greet))

    def exchange(k, src):
        for rel in PARTNERS:
            m = peer(rel)
            send(src.at[:, eight(m), :], gath.at[k, eight(n)], sa.at[k], ra.at[k], (w, m))

    exchange(0, pops)

    for copy in small[:4]:
        copy.wait()
    row = iota((8, 128), 0)
    ca = jnp.zeros((8, 128), F32)
    cb = jnp.zeros((8, 128), F32)
    for i in range(8):
        ca = jnp.where(row == i, coef_s[i], ca)
        cb = jnp.where(row == i, rate_s[i], cb)
    ep[0, n] = ca
    ep[1, n] = ca * cb
    ep[2, n] = msf_v[...]
    ep[3, n] = msf_v[...] * pri_v[...]
    for rel in PARTNERS:
        send(ep.at[:, n], ep.at[:, n], se.at[0], re.at[0], (w, peer(rel)))

    for copy in small[4:9]:
        copy.wait()
    kt_high, kt_low = split(kct_v[...])
    kt = jnp.concatenate([kt_high, kt_low, kt_high, kt_low], axis=0).astype(F32)
    kmat[...] = kt.T.astype(BF16)
    s_high, s_low = split(sto_v[...])
    smat[...] = jnp.concatenate(
        [jnp.concatenate([s_high, s_high], 1), jnp.concatenate([s_low, s_low], 1)], axis=0
    )
    place = iota((256, 128), 0)
    own = iota((256, 128), 1)
    inside = jnp.where(place >= 128, place - 128, place)
    inside = jnp.where(inside >= 64, inside - 64, inside)
    for k in range(2):
        for part in range(2):
            if part == 0:
                named = inside + jnp.where(place < 128, 64, 0)
            else:
                named = inside + 128
            table = jnp.zeros((256, 128), F32)
            for j in range(4):
                pad = jnp.zeros((1, 64), jnp.int32)
                near = jnp.concatenate([adj_v[j : j + 1, :] - (w * 64 - 64), pad], axis=1)
                tally = jnp.concatenate([tal_v[k, j : j + 1, :], pad], axis=1)
                weight = tally.astype(F32) * 0.5
                table = table + jnp.where(named == near, weight, 0.0)
                if part == 0:
                    table = table - jnp.where(named == own + 64, weight, 0.0)
            wmat[k, part] = table.T[:64].astype(BF16)

    wait(ep.at[:, 0:7], re.at[0])
    send(ep.at[2], msfh.at[1], se.at[1], re.at[1], (left, n))
    send(ep.at[2], msfh.at[0], se.at[2], re.at[2], (right, n))

    def tables(b, carry):
        node = tgt_v[pl.ds(b, 1), :]
        low = lax.rem(node, 128)
        high = lax.rem(node // 128, 8) * 8 + node // 1024
        lot[b] = jnp.where(iota((128, 128), 0) == low, 1.0, 0.0).astype(BF16)
        him[b] = jnp.where(iota((64, 128), 0) == high, 1.0, 0.0).astype(BF16)
        return carry

    lax.fori_loop(0, 64, tables, 0)

    def chemistry(k):
        wait(draws_v.at[k], dloc.at[k])
        populations = gath.at[k].reshape(512, 128)
        reacted = react.at[k].reshape(512, 128)
        for pair in range(4):
            blocks = (2 * pair, 2 * pair + 1)
            p = jnp.concatenate([populations[pl.ds(b, 64, stride=8), :] for b in blocks], axis=1)
            high, low = split(p)
            propensity = dot(kmat[...], jnp.concatenate([high, high, low, low], axis=0))
            d = jnp.concatenate([draws_v[k, b] for b in blocks], axis=1)
            fired = propensity * (d.astype(F32) * (1.0 / 3.5))
            change = dot(smat[...], jnp.concatenate(split(fired), axis=0))
            p = p + 0.25 * (change[:64] + change[64:])
            for i, b in enumerate(blocks):
                reacted[pl.ds(b, 64, stride=8), :] = p[:, 128 * i : 128 * i + 128]

    def chunk(k, side, m):
        return halo.at[k, pl.ds(8 * side, 8), eight(m), :]

    def send_reacted(k):
        for rel in PARTNERS:
            m = peer(rel)
            send(
                react.at[k, eight(m)], chunk(k, 1, n), sh.at[k], r2.at[k, PARTNERS.index(rel)], (w, m)
            )
        for rel in ((0, 0),) + DIRECT:
            m = peer(rel)
            slot = 7 if rel == (0, 0) else PARTNERS.index(rel)
            send(react.at[k, eight(m)], chunk(k, 2, n), sh.at[k], rh.at[k, 1, slot], (left, m))
            send(react.at[k, eight(m)], chunk(k, 0, n), sh.at[k], rh.at[k, 0, slot], (right, m))
        halo[k, 8:16, eight(n), :] = react[k, eight(n)]

    def forward_reacted(k):
        for i, rel in enumerate(PARTNERS):
            if rel in DIRECT:
                continue
            m = source(rel)
            wait(chunk(k, 1, m), r2.at[k, i])
            send(chunk(k, 1, m), chunk(k, 2, m), sh.at[k], rh.at[k, 1, i], (left, n))
            send(chunk(k, 1, m), chunk(k, 0, m), sh.at[k], rh.at[k, 0, i], (right, n))

    def wait_reacted(k):
        for i, rel in enumerate(PARTNERS):
            if rel in DIRECT:
                wait(chunk(k, 1, source(rel)), r2.at[k, i])
        for i, rel in enumerate(PARTNERS + ((0, 0),)):
            for side in (0, 1):
                wait(chunk(k, 2 * side, source(rel)), rh.at[k, side, i])

    def diffuse(k):
        for pair in range(4):
            parts = [
                split(
                    jnp.concatenate(
                        [halo[k, 8 * side + 2 * pair + i] for i in range(2)], axis=1
                    )
                )
                for side in (1, 0, 2)
            ]
            first = jnp.concatenate(parts[0] + parts[1], axis=0)
            second = jnp.concatenate(parts[2], axis=0)
            flux = dot(wmat[k, 0], first) + dot(wmat[k, 1, :, :128], second)
            for i in range(2):
                s = 2 * pair + i
                diff[k, s] = halo[k, 8 + s] + rate_s[s] * flux[:, 128 * i : 128 * i + 128]

    wait(gath.at[0, 0:56], ra.at[0])
    small[9].wait()
    chemistry(0)
    send_reacted(0)
    forward_reacted(0)
    wait_reacted(0)
    diffuse(0)
    exchange(1, diff.at[0])
    gath[1, eight(n)] = diff[0, :, eight(n), :]

    wait(gath.at[1, 0:56], ra.at[1])
    chemistry(1)
    u = jnp.zeros((8, 128), F32)
    v = jnp.zeros((8, 128), F32)
    for s in range(64):
        tile = react[1, s]
        u = u + ep[0, s // 8, s % 8 : s % 8 + 1, :] * tile
        v = v + ep[1, s // 8, s % 8 : s % 8 + 1, :] * tile
    uv[2, eight(n)] = v
    uv[3, eight(n)] = u
    for rel in PARTNERS:
        mine = uv.at[2:4, eight(n), :]
        send(mine, mine, su.at[0], ru.at[0], (w, peer(rel)))
    for rel in PARTNERS + ((0, 0),):
        send(uv.at[2, eight(n)], uv.at[1, eight(n)], su.at[1], ru.at[1], (left, peer(rel)))
        send(uv.at[2, eight(n)], uv.at[0, eight(n)], su.at[1], ru.at[1], (right, peer(rel)))
    send_reacted(1)

    wait(uv.at[2:4, 0:56, :], ru.at[0])
    wait(uv.at[0:2], ru.at[1])
    vs, vl, vr = split(uv[2]), split(uv[0]), split(uv[1])
    current = (
        uv[3]
        + dot(wmat[1, 0], jnp.concatenate(vs + vl, axis=0))
        + dot(wmat[1, 1, :, :128], jnp.concatenate(vr, axis=0))
    )
    c_high, c_low = split(current)
    total = jnp.zeros((128, 128), F32)
    for pair in range(32):
        rows, columns = [], []
        for b in (2 * pair, 2 * pair + 1):
            mask = him[b]
            rows.append(
                jnp.concatenate([mask * c_high[b : b + 1], mask * c_low[b : b + 1]], axis=0)
            )
            columns.append(lot[b])
        total = total + dot_nt(jnp.concatenate(rows, axis=1), jnp.concatenate(columns, axis=1))
    total = total[:64] + total[64:]
    for c in range(8):
        vh[1, c] = ep[3, c] + total[8 * c : 8 * c + 8]
    send(vh.at[1], vh.at[2], sg.at[0], rg.at[0], (left, n))
    send(vh.at[1], vh.at[0], sg.at[1], rg.at[1], (right, n))
    forward_reacted(1)

    wait(msfh.at[0], re.at[1])
    wait(msfh.at[0], re.at[2])
    wait(vh.at[2], rg.at[0])
    wait(vh.at[0], rg.at[1])

    def wide_rows(parts):
        return jnp.concatenate(
            [jnp.concatenate([part[c] for c in range(8)], axis=1) for part in parts], axis=0
        )

    rows24 = iota((24, 1024), 0)
    columns24 = iota((24, 1024), 1)
    outside = ((w == 0) & (rows24 < 8)) | ((w == wides - 1) & (rows24 >= 16))
    factor = wide_rows([msfh.at[0], ep.at[2], msfh.at[1]])
    vector = jnp.where(outside, 0.0, wide_rows([vh.at[0], vh.at[1], vh.at[2]]))
    vectors = [vector]
    for step in range(3):
        beside = pltpu.roll(vector, 1, 0) + pltpu.roll(vector, 23, 0)
        beside = beside + jnp.where(columns24 == 0, 0.0, pltpu.roll(vector, 1, 1))
        beside = beside + jnp.where(columns24 == 1023, 0.0, pltpu.roll(vector, 1023, 1))
        vector = jnp.where(outside, 0.0, ((4.0 - SHIFT) + factor) * vector - beside)
        vectors.append(vector)
    vectors = [v[8:16] for v in vectors]
    for k in range(3):
        for c in range(8):
            fields[k, c] = vectors[k][:, 128 * c : 128 * c + 128]
    sums = []
    for k in range(6):
        product = vectors[k // 2] * vectors[(k + 1) // 2]
        tile = product[:, :128]
        for c in range(1, 8):
            tile = tile + product[:, 128 * c : 128 * c + 128]
        sums.append(jnp.sum(tile, axis=0, keepdims=True))
    mz[z] = jnp.concatenate(sums + [jnp.zeros((2, 128), F32)], axis=0)
    for to in z_line:
        send(mz.at[z], mz.at[z], so.at[0], so.at[1], (to, n))

    wait_reacted(1)
    diffuse(1)
    amounts = pltpu.make_async_copy(diff.at[1], out_pops, loc.at[10])
    amounts.start()

    wait(mz.at[0 : zs - 1], so.at[1])
    mx[x] = jnp.sum(mz[...], axis=0)
    for to in x_line:
        send(mx.at[x], mx.at[x], so.at[2], so.at[3], (to, n))
    wait(mx.at[0 : xs - 1], so.at[3])
    sums = jnp.sum(jnp.sum(mx[...], axis=0), axis=1, keepdims=True)
    a, b, c = krylov_coefficients([sums[k : k + 1] for k in range(6)])
    msf_v[...] = a * fields[0, n] + b * fields[1, n] + c * fields[2, n]
    voltage = pltpu.make_async_copy(msf_v, out_pot, loc.at[11])
    voltage.start()

    for k in range(2):
        wait(gath.at[k, 0:56], sa.at[k])
        wait(halo.at[k, 0:23], sh.at[k])
    wait(ep.at[:, 0:7], se.at[0])
    wait(msfh.at[0], se.at[1])
    wait(msfh.at[0], se.at[2])
    wait(uv.at[2:4, 0:56, :], su.at[0])
    wait(uv.at[0:2], su.at[1])
    wait(vh.at[0], sg.at[0])
    wait(vh.at[0], sg.at[1])
    wait(mz.at[0 : zs - 1], so.at[0])
    wait(mx.at[0 : xs - 1], so.at[2])
    amounts.wait()
    voltage.wait()


def solution(mesh):
    zs = 8
    xs = mesh.shape["wide"] // zs

    def shards(pops, kinetic, sto, draws, rates, adjacency, tallies, coef, target, msf, prior):
        any_spec = pl.BlockSpec(memory_space=pl.ANY)
        dma = pltpu.SemaphoreType.DMA
        vmem = pltpu.VMEM
        return pl.pallas_call(
            functools.partial(kernel, zs, xs),
            out_shape=(
                jax.ShapeDtypeStruct(pops.shape, F32),
                jax.ShapeDtypeStruct(msf.shape, F32),
            ),
            in_specs=[any_spec] * 11,
            out_specs=(any_spec, any_spec),
            scratch_shapes=[
                vmem((2, 64, 8, 128), F32),
                vmem((2, 64, 8, 128), F32),
                vmem((2, 24, 64, 128), F32),
                vmem((2, 8, 64, 128), F32),
                vmem((2, 8, 128, 128), jnp.int32),
                vmem((64, 128), F32),
                vmem((64, 128), F32),
                vmem((4, 64), jnp.int32),
                vmem((2, 4, 64), jnp.int32),
                vmem((64, 128), jnp.int32),
                vmem((8, 128), F32),
                vmem((8, 128), F32),
                pltpu.SMEM((8,), F32),
                pltpu.SMEM((8,), F32),
                vmem((4, 8, 8, 128), F32),
                vmem((2, 8, 8, 128), F32),
                vmem((128, 256), BF16),
                vmem((128, 256), BF16),
                vmem((2, 2, 64, 256), BF16),
                vmem((64, 128, 128), BF16),
                vmem((64, 64, 128), BF16),
                vmem((4, 64, 128), F32),
                vmem((3, 8, 8, 128), F32),
                vmem((3, 8, 8, 128), F32),
                vmem((zs, 8, 128), F32),
                vmem((xs, 8, 128), F32),
                dma((12,)),
                dma((2,)),
                dma((2,)),
                dma((2,)),
                dma((2,)),
                dma((2, 7)),
                dma((2, 2, 8)),
                dma((3,)),
                dma((3,)),
                dma((2,)),
                dma((2,)),
                dma((2,)),
                dma((2,)),
                dma((4,)),
            ],
            compiler_params=pltpu.CompilerParams(
                collective_id=0, has_side_effects=True, vmem_limit_bytes=48 * 1024 * 1024
            ),
        )(
            pops, kinetic.T, sto, draws, rates, adjacency.T, tallies.transpose(0, 2, 1), coef,
            target, msf, prior,
        )

    return jax.shard_map(
        shards,
        mesh=mesh,
        in_specs=(
            P("narrow", "wide", None),
            P(),
            P(),
            P(None, None, ("wide", "narrow"), None),
            P("narrow"),
            P("wide", None),
            P(None, "wide", None),
            P("narrow"),
            P("wide", None),
            P("wide", "narrow"),
            P("wide", "narrow"),
        ),
        out_specs=(P("narrow", "wide", None), P("wide", "narrow")),
        check_vma=False,
    )
```

```python
import functools

import jax
import jax.numpy as jnp
from jax import lax
from jax.experimental import pallas as pl
from jax.experimental.pallas import tpu as pltpu
from jax.sharding import PartitionSpec as P

MESH = pl.DeviceIdType.MESH
F32 = jnp.float32
BF16 = jnp.bfloat16

PARTNERS = ((1, 0), (3, 0), (1, 1), (3, 1), (2, 0), (2, 1), (0, 1))
DIRECT = PARTNERS
SHIFT = 4.0
VLIM = 62
HALF = (4, 8)


def split(x):
    high = x.astype(BF16)
    return high, (x - high.astype(F32)).astype(BF16)


def dot(a, b):
    return jnp.dot(a, b, preferred_element_type=F32)


def dot_nt(a, b):
    return lax.dot_general(a, b, (((1,), (1,)), ((), ())), preferred_element_type=F32)


def iota(shape, dim):
    return lax.broadcasted_iota(jnp.int32, shape, dim)


def inner(p, q, moments):
    total = None
    for i, pi in enumerate(p):
        for j, qj in enumerate(q):
            term = pi * qj * moments[i + j]
            total = term if total is None else total + term
    return total


def krylov_coefficients(moments):
    one = jnp.ones_like(moments[0])
    direction, residual = [one], [one]
    x = [jnp.zeros_like(one)] * 3
    norm = moments[0]
    for iteration in range(3):
        size = len(direction)
        applied = [SHIFT * d for d in direction] + [jnp.zeros_like(one)]
        for i in range(size):
            applied[i + 1] = applied[i + 1] + direction[i]
        step = norm / inner(direction, applied, moments)
        x = [x[i] + step * direction[i] if i < size else x[i] for i in range(3)]
        if iteration == 2:
            return x
        residual = [
            (residual[i] if i < len(residual) else 0.0) - step * applied[i] for i in range(size + 1)
        ]
        fresh = inner(residual, residual, moments)
        ratio = fresh / norm
        norm = fresh
        direction = [
            residual[i] + ratio * direction[i] if i < size else residual[i] for i in range(size + 1)
        ]


def kernel(
    zs, xs,
    pops, kct, sto, draws, rates, adjt, talt, coef, tgt, msf, prior,
    out_pops, out_pot,
    gath, react, halo, diff, draws_v, kct_v, sto_v, adj_v, tal_v, tgt_v, msf_v, pri_v,
    rate_s, coef_s, ep, msfh, kmat, smat, wmat, lot, him, uv, vh, fields, mz,
    loc, dloc, sa, ra, sh, r2, rh, se, re, su, ru, sg, rg, so,
):
    w, n = lax.axis_index("wide"), lax.axis_index("narrow")
    wides = zs * xs
    left, right = lax.rem(w + wides - 1, wides), lax.rem(w + 1, wides)
    y, core = n // 2, lax.rem(n, 2)
    x, z = w // zs, lax.rem(w, zs)

    def peer(rel):
        return lax.rem(y + rel[0], 4) * 2 + lax.rem(core + rel[1], 2)

    def source(rel):
        return peer(((4 - rel[0]) % 4, rel[1]))

    def eight(i):
        return pl.ds(pl.multiple_of(i * 8, 8), 8)

    def send(src, dst, s, r, to):
        pltpu.make_async_remote_copy(
            src_ref=src, dst_ref=dst, send_sem=s, recv_sem=r, device_id=to, device_id_type=MESH
        ).start()

    def wait(ref, sem):
        pltpu.make_async_copy(ref, ref, sem).wait()

    steps = [(i, j) for i in range(xs) for j in range(zs)][1:]
    steps.sort(key=lambda s: -(min(s[0], xs - s[0]) + min(s[1], zs - s[1])))
    others = [lax.rem(x + i, xs) * zs + lax.rem(z + j, zs) for i, j in steps]

    barrier = pltpu.get_barrier_semaphore()
    greet = [(w, peer(rel)) for rel in PARTNERS]
    for side in (left, right):
        greet += [(side, n)] + [(side, peer(rel)) for rel in PARTNERS]
    greet += [(v, n) for v in others]
    for to in greet:
        pl.semaphore_signal(barrier, inc=1, device_id=to, device_id_type=MESH)

    small = [
        (coef, coef_s), (rates, rate_s), (msf, msf_v), (prior, pri_v), (kct, kct_v), (sto, sto_v),
        (adjt, adj_v), (talt, tal_v), (tgt, tgt_v), (pops.at[:, eight(n), :], gath.at[0, eight(n)]),
    ]
    small = [pltpu.make_async_copy(s, d, loc.at[i]) for i, (s, d) in enumerate(small)]
    for copy in small:
        copy.start()
    for k in range(2):
        for b in range(8):
            pltpu.make_async_copy(draws.at[k, :, b, :], draws_v.at[k, b], dloc.at[k]).start()
    pl.semaphore_wait(barrier, len(greet))

    for rel in PARTNERS:
        m = peer(rel)
        send(pops.at[:, eight(m), :], gath.at[0, eight(n)], sa.at[0], ra.at[0], (w, m))


    for copy in small[:4]:
        copy.wait()
    row = iota((8, 128), 0)
    ca = jnp.zeros((8, 128), F32)
    cb = jnp.zeros((8, 128), F32)
    for i in range(8):
        ca = jnp.where(row == i, coef_s[i], ca)
        cb = jnp.where(row == i, rate_s[i], cb)
    ep[0, n] = ca
    ep[1, n] = ca * cb
    ep[2, n] = msf_v[...]
    ep[3, n] = msf_v[...] * pri_v[...]
    for rel in PARTNERS:
        send(ep.at[:, n], ep.at[:, n], se.at[0], re.at[0], (w, peer(rel)))

    for copy in small[4:9]:
        copy.wait()
    kt_high, kt_low = split(kct_v[...])
    kt = jnp.concatenate([kt_high, kt_low, kt_high, kt_low], axis=0).astype(F32)
    kmat[...] = kt.T.astype(BF16)
    s_high, s_low = split(sto_v[...])
    smat[...] = jnp.concatenate(
        [jnp.concatenate([s_high, s_high], 1), jnp.concatenate([s_low, s_low], 1)], axis=0
    )
    def tables(b, carry):
        node = tgt_v[pl.ds(b, 1), :]
        low = lax.rem(node, 128)
        high = lax.rem(node // 128, 8) * 8 + node // 1024
        lot[b] = jnp.where(iota((128, 128), 0) == low, 1.0, 0.0).astype(BF16)
        him[b] = jnp.where(iota((64, 128), 0) == high, 1.0, 0.0).astype(BF16)
        return carry

    def hop_tables():
        place = iota((256, 128), 0)
        own = iota((256, 128), 1)
        inside = jnp.where(place >= 128, place - 128, place)
        inside = jnp.where(inside >= 64, inside - 64, inside)
        for k in range(2):
            for part in range(2):
                if part == 0:
                    named = inside + jnp.where(place < 128, 64, 0)
                else:
                    named = inside + 128
                table = jnp.zeros((256, 128), F32)
                for j in range(4):
                    pad = jnp.zeros((1, 64), jnp.int32)
                    near = jnp.concatenate([adj_v[j : j + 1, :] - (w * 64 - 64), pad], axis=1)
                    tally = jnp.concatenate([tal_v[k, j : j + 1, :], pad], axis=1)
                    weight = tally.astype(F32) * 0.5
                    table = table + jnp.where(named == near, weight, 0.0)
                    if part == 0:
                        table = table - jnp.where(named == own + 64, weight, 0.0)
                wmat[k, part] = table.T[:64].astype(BF16)


    def chemistry(k):
        wait(draws_v.at[k], dloc.at[k])
        populations = gath.at[k].reshape(512, 128)
        reacted = react.at[k].reshape(512, 128)
        for pair in range(4):
            blocks = (2 * pair, 2 * pair + 1)
            p = jnp.concatenate([populations[pl.ds(b, 64, stride=8), :] for b in blocks], axis=1)
            high, low = split(p)
            propensity = dot(kmat[...], jnp.concatenate([high, high, low, low], axis=0))
            d = jnp.concatenate([draws_v[k, b] for b in blocks], axis=1)
            fired = propensity * (d.astype(F32) * (1.0 / 3.5))
            change = dot(smat[...], jnp.concatenate(split(fired), axis=0))
            p = p + 0.25 * (change[:64] + change[64:])
            for i, b in enumerate(blocks):
                reacted[pl.ds(b, 64, stride=8), :] = p[:, 128 * i : 128 * i + 128]

    def chunk(k, side, m, h):
        return halo.at[k, pl.ds(8 * side + HALF[k] * h, HALF[k]), eight(m), :]

    def send_reacted(k, h):
        def reacted(m):
            return react.at[k, pl.ds(pl.multiple_of(8 * m + HALF[k] * h, HALF[k]), HALF[k])]

        for i, rel in enumerate(PARTNERS):
            m = peer(rel)
            send(reacted(m), chunk(k, 1, n, h), sh.at[k], r2.at[k, h, i], (w, m))
        for rel in ((0, 0),) + DIRECT:
            m = peer(rel)
            slot = 7 if rel == (0, 0) else PARTNERS.index(rel)
            send(reacted(m), chunk(k, 2, n, h), sh.at[k], rh.at[k, h, 1, slot], (left, m))
            send(reacted(m), chunk(k, 0, n, h), sh.at[k], rh.at[k, h, 0, slot], (right, m))

    def keep_reacted(k):
        halo[k, 8:16, eight(n), :] = react[k, eight(n)]

    def forward_reacted(k, h):
        for i, rel in enumerate(PARTNERS):
            if rel in DIRECT:
                continue
            m = source(rel)
            wait(chunk(k, 1, m, h), r2.at[k, h, i])
            send(chunk(k, 1, m, h), chunk(k, 2, m, h), sh.at[k], rh.at[k, h, 1, i], (left, n))
            send(chunk(k, 1, m, h), chunk(k, 0, m, h), sh.at[k], rh.at[k, h, 0, i], (right, n))

    def wait_reacted(k, h):
        for i, rel in enumerate(PARTNERS):
            if rel in DIRECT:
                wait(chunk(k, 1, source(rel), h), r2.at[k, h, i])
        for i, rel in enumerate(PARTNERS + ((0, 0),)):
            for side in (0, 1):
                wait(chunk(k, 2 * side, source(rel), h), rh.at[k, h, side, i])

    def diffuse(k, h):
        for pair in range(HALF[k] // 2 * h, HALF[k] // 2 * (h + 1)):
            parts = [
                split(
                    jnp.concatenate(
                        [halo[k, 8 * side + 2 * pair + i] for i in range(2)], axis=1
                    )
                )
                for side in (1, 0, 2)
            ]
            first = jnp.concatenate(parts[0] + parts[1], axis=0)
            second = jnp.concatenate(parts[2], axis=0)
            flux = dot(wmat[k, 0], first) + dot(wmat[k, 1, :, :128], second)
            for i in range(2):
                s = 2 * pair + i
                diff[k, s] = halo[k, 8 + s] + rate_s[s] * flux[:, 128 * i : 128 * i + 128]

    wait(gath.at[0, 0:56], ra.at[0])
    small[9].wait()
    chemistry(0)
    for h in range(8 // HALF[0]):
        send_reacted(0, h)
    keep_reacted(0)
    hop_tables()
    for h in range(8 // HALF[0]):
        forward_reacted(0, h)
    lax.fori_loop(0, 24, tables, 0)
    for h in range(8 // HALF[0]):
        wait_reacted(0, h)
        diffuse(0, h)
        for rel in PARTNERS:
            m = peer(rel)
            send(
                diff.at[0, pl.ds(HALF[0] * h, HALF[0]), eight(m), :],
                gath.at[1, pl.ds(pl.multiple_of(8 * n + HALF[0] * h, HALF[0]), HALF[0])],
                sa.at[1], ra.at[1], (w, m),
            )
    gath[1, eight(n)] = diff[0, :, eight(n), :]
    lax.fori_loop(24, 64, tables, 0)
    wait(ep.at[:, 0:7], re.at[0])
    send(ep.at[2], msfh.at[1], se.at[1], re.at[1], (left, n))
    send(ep.at[2], msfh.at[0], se.at[2], re.at[2], (right, n))


    wait(gath.at[1, 0:56], ra.at[1])
    chemistry(1)
    u = jnp.zeros((8, 128), F32)
    v = jnp.zeros((8, 128), F32)
    for s in range(64):
        tile = react[1, s]
        u = u + ep[0, s // 8, s % 8 : s % 8 + 1, :] * tile
        v = v + ep[1, s // 8, s % 8 : s % 8 + 1, :] * tile
    uv[2, eight(n)] = v
    uv[3, eight(n)] = u
    for rel in PARTNERS + ((0, 0),):
        send(uv.at[2, eight(n)], uv.at[1, eight(n)], su.at[1], ru.at[1], (left, peer(rel)))
        send(uv.at[2, eight(n)], uv.at[0, eight(n)], su.at[1], ru.at[1], (right, peer(rel)))
    for rel in PARTNERS:
        mine = uv.at[2:4, eight(n), :]
        send(mine, mine, su.at[0], ru.at[0], (w, peer(rel)))
    send_reacted(1, 0)
    keep_reacted(1)

    wait(uv.at[2:4, 0:56, :], ru.at[0])
    wait(uv.at[0:2], ru.at[1])
    vs, vl, vr = split(uv[2]), split(uv[0]), split(uv[1])
    current = (
        uv[3]
        + dot(wmat[1, 0], jnp.concatenate(vs + vl, axis=0))
        + dot(wmat[1, 1, :, :128], jnp.concatenate(vr, axis=0))
    )
    c_high, c_low = split(current)
    total = jnp.zeros((128, 128), F32)
    for pair in range(32):
        rows, columns = [], []
        for b in (2 * pair, 2 * pair + 1):
            mask = him[b]
            rows.append(
                jnp.concatenate([mask * c_high[b : b + 1], mask * c_low[b : b + 1]], axis=0)
            )
            columns.append(lot[b])
        total = total + dot_nt(jnp.concatenate(rows, axis=1), jnp.concatenate(columns, axis=1))
    total = total[:64] + total[64:]
    for c in range(8):
        vh[1, c] = ep[3, c] + total[8 * c : 8 * c + 8]
    send(vh.at[1], vh.at[2], sg.at[0], rg.at[0], (left, n))
    send(vh.at[1], vh.at[0], sg.at[1], rg.at[1], (right, n))
    forward_reacted(1, 0)

    wait(msfh.at[0], re.at[1])
    wait(msfh.at[0], re.at[2])
    wait(vh.at[2], rg.at[0])
    wait(vh.at[0], rg.at[1])

    def wide_rows(parts):
        return jnp.concatenate(
            [jnp.concatenate([part[c] for c in range(8)], axis=1) for part in parts], axis=0
        )

    rows24 = iota((24, 1024), 0)
    columns24 = iota((24, 1024), 1)
    outside = ((w == 0) & (rows24 < 8)) | ((w == wides - 1) & (rows24 >= 16))
    factor = wide_rows([msfh.at[0], ep.at[2], msfh.at[1]])
    vector = jnp.where(outside, 0.0, wide_rows([vh.at[0], vh.at[1], vh.at[2]]))
    vectors = [vector]
    for step in range(3):
        beside = pltpu.roll(vector, 1, 0) + pltpu.roll(vector, 23, 0)
        beside = beside + jnp.where(columns24 == 0, 0.0, pltpu.roll(vector, 1, 1))
        beside = beside + jnp.where(columns24 == 1023, 0.0, pltpu.roll(vector, 1023, 1))
        vector = jnp.where(outside, 0.0, ((4.0 - SHIFT) + factor) * vector - beside)
        vectors.append(vector)
    vectors = [v[8:16] for v in vectors]
    for k in range(3):
        for c in range(8):
            fields[k, c] = vectors[k][:, 128 * c : 128 * c + 128]
    sums = []
    for k in range(6):
        product = vectors[k // 2] * vectors[(k + 1) // 2]
        tile = product[:, :128]
        for c in range(1, 8):
            tile = tile + product[:, 128 * c : 128 * c + 128]
        sums.append(jnp.sum(tile, axis=0, keepdims=True))
    tile = jnp.concatenate(sums + [jnp.zeros((2, 128), F32)], axis=0)
    tile = jnp.sum(tile, axis=1, keepdims=True)
    diagonal = iota((8, 128), 0) == iota((8, 128), 1)
    mz[w] = jnp.sum(jnp.where(diagonal, tile, 0.0), axis=0, keepdims=True)
    for to in others:
        send(mz.at[w], mz.at[w], so.at[0], so.at[1], (to, n))

    wait_reacted(1, 0)
    diffuse(1, 0)
    amounts = pltpu.make_async_copy(diff.at[1], out_pops, loc.at[10])
    amounts.start()

    wait(mz.at[0 : wides - 1], so.at[1])
    tile = jnp.sum(mz[...].reshape(wides, 128), axis=0, keepdims=True)
    sums = jnp.sum(jnp.where(diagonal, tile, 0.0), axis=1, keepdims=True)
    a, b, c = krylov_coefficients([sums[k : k + 1] for k in range(6)])
    msf_v[...] = a * fields[0, n] + b * fields[1, n] + c * fields[2, n]
    voltage = pltpu.make_async_copy(msf_v, out_pot, loc.at[11])
    voltage.start()

    for k in range(2):
        wait(gath.at[k, 0:56], sa.at[k])
        wait(halo.at[k, 0:23], sh.at[k])
    wait(ep.at[:, 0:7], se.at[0])
    wait(msfh.at[0], se.at[1])
    wait(msfh.at[0], se.at[2])
    wait(uv.at[2:4, 0:56, :], su.at[0])
    wait(uv.at[0:2], su.at[1])
    wait(vh.at[0], sg.at[0])
    wait(vh.at[0], sg.at[1])
    wait(mz.at[0 : wides - 1], so.at[0])
    amounts.wait()
    voltage.wait()


def solution(mesh):
    zs = 8
    xs = mesh.shape["wide"] // zs

    def shards(pops, kinetic, sto, draws, rates, adjacency, tallies, coef, target, msf, prior):
        any_spec = pl.BlockSpec(memory_space=pl.ANY)
        hbm_spec = pl.BlockSpec(memory_space=pltpu.HBM)
        dma = pltpu.SemaphoreType.DMA
        vmem = pltpu.VMEM
        return pl.pallas_call(
            functools.partial(kernel, zs, xs),
            out_shape=(
                pltpu.VMEM(pops.shape, F32),
                pltpu.VMEM(msf.shape, F32),
            ),
            in_specs=[hbm_spec] * 11,
            out_specs=(any_spec, any_spec),
            scratch_shapes=[
                vmem((2, 64, 8, 128), F32),
                vmem((2, 64, 8, 128), F32),
                vmem((2, 24, 64, 128), F32),
                vmem((2, 8, 64, 128), F32),
                vmem((2, 8, 128, 128), jnp.int32),
                vmem((64, 128), F32),
                vmem((64, 128), F32),
                vmem((4, 64), jnp.int32),
                vmem((2, 4, 64), jnp.int32),
                vmem((64, 128), jnp.int32),
                vmem((8, 128), F32),
                vmem((8, 128), F32),
                pltpu.SMEM((8,), F32),
                pltpu.SMEM((8,), F32),
                vmem((4, 8, 8, 128), F32),
                vmem((2, 8, 8, 128), F32),
                vmem((128, 256), BF16),
                vmem((128, 256), BF16),
                vmem((2, 2, 64, 256), BF16),
                vmem((64, 128, 128), BF16),
                vmem((64, 64, 128), BF16),
                vmem((4, 64, 128), F32),
                vmem((3, 8, 8, 128), F32),
                vmem((3, 8, 8, 128), F32),
                vmem((zs * xs, 1, 128), F32),
                dma((12,)),
                dma((2,)),
                dma((2,)),
                dma((2,)),
                dma((2,)),
                dma((2, 4, 7)),
                dma((2, 4, 2, 8)),
                dma((3,)),
                dma((3,)),
                dma((2,)),
                dma((2,)),
                dma((2,)),
                dma((2,)),
                dma((2,)),
            ],
            compiler_params=pltpu.CompilerParams(
                collective_id=0, has_side_effects=True, vmem_limit_bytes=VLIM * 1024 * 1024
            ),
        )(
            pops, kinetic.T, sto, draws, rates, adjacency.T, tallies.transpose(0, 2, 1), coef,
            target, msf, prior,
        )

    return jax.shard_map(
        shards,
        mesh=mesh,
        in_specs=(
            P("narrow", "wide", None),
            P(),
            P(),
            P(None, None, ("wide", "narrow"), None),
            P("narrow"),
            P("wide", None),
            P(None, "wide", None),
            P("narrow"),
            P("wide", None),
            P("wide", "narrow"),
            P("wide", "narrow"),
        ),
        out_specs=(P("narrow", "wide", None), P("wide", "narrow")),
        check_vma=False,
    )
```

```python
import functools

import jax
import jax.numpy as jnp
from jax import lax
from jax.experimental import pallas as pl
from jax.experimental.pallas import tpu as pltpu
from jax.sharding import PartitionSpec as P

MESH = pl.DeviceIdType.MESH
F32 = jnp.float32
BF16 = jnp.bfloat16

PARTNERS = ((1, 0), (3, 0), (1, 1), (3, 1), (2, 0), (2, 1), (0, 1))
DIRECT = ((0, 1), (1, 0), (3, 0), (1, 1), (3, 1))
SHIFT = 4.0
VLIM = 62
HALF = (4, 8)


def split(x):
    high = x.astype(BF16)
    return high, (x - high.astype(F32)).astype(BF16)


def dot(a, b):
    return jnp.dot(a, b, preferred_element_type=F32)


def dot_nt(a, b):
    return lax.dot_general(a, b, (((1,), (1,)), ((), ())), preferred_element_type=F32)


def iota(shape, dim):
    return lax.broadcasted_iota(jnp.int32, shape, dim)


def inner(p, q, moments):
    total = None
    for i, pi in enumerate(p):
        for j, qj in enumerate(q):
            term = pi * qj * moments[i + j]
            total = term if total is None else total + term
    return total


def krylov_coefficients(moments):
    one = jnp.ones_like(moments[0])
    direction, residual = [one], [one]
    x = [jnp.zeros_like(one)] * 3
    norm = moments[0]
    for iteration in range(3):
        size = len(direction)
        applied = [SHIFT * d for d in direction] + [jnp.zeros_like(one)]
        for i in range(size):
            applied[i + 1] = applied[i + 1] + direction[i]
        step = norm / inner(direction, applied, moments)
        x = [x[i] + step * direction[i] if i < size else x[i] for i in range(3)]
        if iteration == 2:
            return x
        residual = [
            (residual[i] if i < len(residual) else 0.0) - step * applied[i] for i in range(size + 1)
        ]
        fresh = inner(residual, residual, moments)
        ratio = fresh / norm
        norm = fresh
        direction = [
            residual[i] + ratio * direction[i] if i < size else residual[i] for i in range(size + 1)
        ]


def kernel(
    zs, xs,
    pops, kct, sto, draws, rates, adjt, talt, coef, tgt, msf, prior,
    out_pops, out_pot,
    gath, react, halo, diff, draws_v, kct_v, sto_v, adj_v, tal_v, tgt_v, msf_v, pri_v,
    rate_s, coef_s, ep, msfh, kmat, smat, wmat, lot, him, uv, vh, edge, fields, mz,
    loc, dloc, sa, ra, sh, r2, rh, se, re, su, ru, sg, rg, so, near,
):
    w, n = lax.axis_index("wide"), lax.axis_index("narrow")
    wides = zs * xs
    left, right = lax.rem(w + wides - 1, wides), lax.rem(w + 1, wides)
    y, core = n // 2, lax.rem(n, 2)
    x, z = w // zs, lax.rem(w, zs)

    def peer(rel):
        return lax.rem(y + rel[0], 4) * 2 + lax.rem(core + rel[1], 2)

    def source(rel):
        return peer(((4 - rel[0]) % 4, rel[1]))

    def eight(i):
        return pl.ds(pl.multiple_of(i * 8, 8), 8)

    def send(src, dst, s, r, to):
        pltpu.make_async_remote_copy(
            src_ref=src, dst_ref=dst, send_sem=s, recv_sem=r, device_id=to, device_id_type=MESH
        ).start()

    def wait(ref, sem):
        pltpu.make_async_copy(ref, ref, sem).wait()

    steps = [(i, j) for i in range(xs) for j in range(zs)][1:]
    steps.sort(key=lambda s: -(min(s[0], xs - s[0]) + min(s[1], zs - s[1])))
    others = [lax.rem(x + i, xs) * zs + lax.rem(z + j, zs) for i, j in steps]

    barrier = pltpu.get_barrier_semaphore()
    greet = [(w, peer(rel)) for rel in PARTNERS]
    greet += [(left, n), (right, n)]
    for to in greet:
        pl.semaphore_signal(barrier, inc=1, device_id=to, device_id_type=MESH)

    small = [
        (coef, coef_s), (rates, rate_s), (msf, msf_v), (prior, pri_v), (kct, kct_v), (sto, sto_v),
        (adjt, adj_v), (talt, tal_v), (tgt, tgt_v), (pops.at[:, eight(n), :], gath.at[0, eight(n)]),
    ]
    small = [pltpu.make_async_copy(s, d, loc.at[i]) for i, (s, d) in enumerate(small)]
    for copy in small:
        copy.start()
    for k in range(2):
        for b in range(8):
            pltpu.make_async_copy(draws.at[k, :, b, :], draws_v.at[k, b], dloc.at[k]).start()
    pl.semaphore_wait(barrier, len(greet))

    for rel in PARTNERS:
        m = peer(rel)
        send(pops.at[:, eight(m), :], gath.at[0, eight(n)], sa.at[0], ra.at[0], (w, m))


    def reach(level):
        far = 2**level
        for to in (lax.rem(w + far, wides), lax.rem(w + wides - far, wides)):
            pl.semaphore_signal(near.at[level], inc=1, device_id=(to, n), device_id_type=MESH)

    reach(0)

    for copy in small[:4]:
        copy.wait()
    row = iota((8, 128), 0)
    ca = jnp.zeros((8, 128), F32)
    cb = jnp.zeros((8, 128), F32)
    for i in range(8):
        ca = jnp.where(row == i, coef_s[i], ca)
        cb = jnp.where(row == i, rate_s[i], cb)
    ep[0, n] = ca
    ep[1, n] = ca * cb
    ep[2, n] = msf_v[...]
    ep[3, n] = msf_v[...] * pri_v[...]
    for rel in PARTNERS:
        send(ep.at[:, n], ep.at[:, n], se.at[0], re.at[0], (w, peer(rel)))

    for copy in small[4:9]:
        copy.wait()
    kt_high, kt_low = split(kct_v[...])
    kt = jnp.concatenate([kt_high, kt_low, kt_high, kt_low], axis=0).astype(F32)
    kmat[...] = kt.T.astype(BF16)
    s_high, s_low = split(sto_v[...])
    smat[...] = jnp.concatenate(
        [jnp.concatenate([s_high, s_high], 1), jnp.concatenate([s_low, s_low], 1)], axis=0
    )
    def tables(b, carry):
        node = tgt_v[pl.ds(b, 1), :]
        low = lax.rem(node, 128)
        high = lax.rem(node // 128, 8) * 8 + node // 1024
        lot[b] = jnp.where(iota((128, 128), 0) == low, 1.0, 0.0).astype(BF16)
        him[b] = jnp.where(iota((64, 128), 0) == high, 1.0, 0.0).astype(BF16)
        return carry

    def hop_tables():
        place = iota((256, 128), 0)
        own = iota((256, 128), 1)
        inside = jnp.where(place >= 128, place - 128, place)
        inside = jnp.where(inside >= 64, inside - 64, inside)
        for k in range(2):
            for part in range(2):
                if part == 0:
                    named = inside + jnp.where(place < 128, 64, 0)
                else:
                    named = inside + 128
                table = jnp.zeros((256, 128), F32)
                for j in range(4):
                    pad = jnp.zeros((1, 64), jnp.int32)
                    near = jnp.concatenate([adj_v[j : j + 1, :] - (w * 64 - 64), pad], axis=1)
                    tally = jnp.concatenate([tal_v[k, j : j + 1, :], pad], axis=1)
                    weight = tally.astype(F32) * 0.5
                    table = table + jnp.where(named == near, weight, 0.0)
                    if part == 0:
                        table = table - jnp.where(named == own + 64, weight, 0.0)
                wmat[k, part] = table.T[:64].astype(BF16)


    def chemistry(k):
        wait(draws_v.at[k], dloc.at[k])
        populations = gath.at[k].reshape(512, 128)
        reacted = react.at[k].reshape(512, 128)
        for pair in range(4):
            blocks = (2 * pair, 2 * pair + 1)
            p = jnp.concatenate([populations[pl.ds(b, 64, stride=8), :] for b in blocks], axis=1)
            high, low = split(p)
            propensity = dot(kmat[...], jnp.concatenate([high, high, low, low], axis=0))
            d = jnp.concatenate([draws_v[k, b] for b in blocks], axis=1)
            fired = propensity * (d.astype(F32) * (1.0 / 3.5))
            change = dot(smat[...], jnp.concatenate(split(fired), axis=0))
            p = p + 0.25 * (change[:64] + change[64:])
            for i, b in enumerate(blocks):
                reacted[pl.ds(b, 64, stride=8), :] = p[:, 128 * i : 128 * i + 128]

    def chunk(k, side, m, h):
        return halo.at[k, pl.ds(8 * side + HALF[k] * h, HALF[k]), eight(m), :]

    def send_reacted(k, h):
        def reacted(m):
            return react.at[k, pl.ds(pl.multiple_of(8 * m + HALF[k] * h, HALF[k]), HALF[k])]

        for i, rel in enumerate(PARTNERS):
            m = peer(rel)
            send(reacted(m), chunk(k, 1, n, h), sh.at[k], r2.at[k, h, i], (w, m))
        for rel in ((0, 0),) + DIRECT:
            m = peer(rel)
            slot = 7 if rel == (0, 0) else PARTNERS.index(rel)
            send(reacted(m), chunk(k, 2, n, h), sh.at[k], rh.at[k, h, 1, slot], (left, m))
            send(reacted(m), chunk(k, 0, n, h), sh.at[k], rh.at[k, h, 0, slot], (right, m))

    def keep_reacted(k):
        halo[k, 8:16, eight(n), :] = react[k, eight(n)]

    def forward_reacted(k, h):
        for i, rel in enumerate(PARTNERS):
            if rel in DIRECT:
                continue
            m = source(rel)
            wait(chunk(k, 1, m, h), r2.at[k, h, i])
            send(chunk(k, 1, m, h), chunk(k, 2, m, h), sh.at[k], rh.at[k, h, 1, i], (left, n))
            send(chunk(k, 1, m, h), chunk(k, 0, m, h), sh.at[k], rh.at[k, h, 0, i], (right, n))

    def wait_reacted(k, h):
        for i, rel in enumerate(PARTNERS):
            if rel in DIRECT:
                wait(chunk(k, 1, source(rel), h), r2.at[k, h, i])
        for i, rel in enumerate(PARTNERS + ((0, 0),)):
            for side in (0, 1):
                wait(chunk(k, 2 * side, source(rel), h), rh.at[k, h, side, i])

    def diffuse(k, h):
        for pair in range(HALF[k] // 2 * h, HALF[k] // 2 * (h + 1)):
            parts = [
                split(
                    jnp.concatenate(
                        [halo[k, 8 * side + 2 * pair + i] for i in range(2)], axis=1
                    )
                )
                for side in (1, 0, 2)
            ]
            first = jnp.concatenate(parts[0] + parts[1], axis=0)
            second = jnp.concatenate(parts[2], axis=0)
            flux = dot(wmat[k, 0], first) + dot(wmat[k, 1, :, :128], second)
            for i in range(2):
                s = 2 * pair + i
                diff[k, s] = halo[k, 8 + s] + rate_s[s] * flux[:, 128 * i : 128 * i + 128]

    wait(gath.at[0, 0:56], ra.at[0])
    small[9].wait()
    chemistry(0)
    pl.semaphore_wait(near.at[0], 2)
    reach(1)
    for h in range(8 // HALF[0]):
        send_reacted(0, h)
    keep_reacted(0)
    hop_tables()
    for h in range(8 // HALF[0]):
        forward_reacted(0, h)
    pl.semaphore_wait(near.at[1], 2)
    reach(2)
    lax.fori_loop(0, 24, tables, 0)
    for h in range(8 // HALF[0]):
        wait_reacted(0, h)
        diffuse(0, h)
        for rel in PARTNERS:
            m = peer(rel)
            send(
                diff.at[0, pl.ds(HALF[0] * h, HALF[0]), eight(m), :],
                gath.at[1, pl.ds(pl.multiple_of(8 * n + HALF[0] * h, HALF[0]), HALF[0])],
                sa.at[1], ra.at[1], (w, m),
            )
    gath[1, eight(n)] = diff[0, :, eight(n), :]
    pl.semaphore_wait(near.at[2], 2)
    reach(3)
    lax.fori_loop(24, 64, tables, 0)
    wait(ep.at[:, 0:7], re.at[0])
    send(ep.at[2], msfh.at[1], se.at[1], re.at[1], (left, n))
    send(ep.at[2], msfh.at[0], se.at[2], re.at[2], (right, n))


    wait(gath.at[1, 0:56], ra.at[1])
    chemistry(1)
    u = jnp.zeros((8, 128), F32)
    v = jnp.zeros((8, 128), F32)
    for s in range(64):
        tile = react[1, s]
        u = u + ep[0, s // 8, s % 8 : s % 8 + 1, :] * tile
        v = v + ep[1, s // 8, s % 8 : s % 8 + 1, :] * tile
    uv[2, eight(n)] = v
    uv[3, eight(n)] = u
    for rel in PARTNERS + ((0, 0),):
        send(uv.at[2, eight(n)], uv.at[1, eight(n)], su.at[1], ru.at[1], (left, peer(rel)))
        send(uv.at[2, eight(n)], uv.at[0, eight(n)], su.at[1], ru.at[1], (right, peer(rel)))
    for rel in PARTNERS:
        mine = uv.at[2:4, eight(n), :]
        send(mine, mine, su.at[0], ru.at[0], (w, peer(rel)))
    send_reacted(1, 0)
    keep_reacted(1)
    pl.semaphore_wait(near.at[3], 2)

    wait(uv.at[2:4, 0:56, :], ru.at[0])
    wait(uv.at[0:2], ru.at[1])
    vs, vl, vr = split(uv[2]), split(uv[0]), split(uv[1])
    current = (
        uv[3]
        + dot(wmat[1, 0], jnp.concatenate(vs + vl, axis=0))
        + dot(wmat[1, 1, :, :128], jnp.concatenate(vr, axis=0))
    )
    c_high, c_low = split(current)
    total = jnp.zeros((128, 128), F32)
    for pair in range(32):
        rows, columns = [], []
        for b in (2 * pair, 2 * pair + 1):
            mask = him[b]
            rows.append(
                jnp.concatenate([mask * c_high[b : b + 1], mask * c_low[b : b + 1]], axis=0)
            )
            columns.append(lot[b])
        total = total + dot_nt(jnp.concatenate(rows, axis=1), jnp.concatenate(columns, axis=1))
    total = total[:64] + total[64:]
    for c in range(8):
        vh[1, c] = ep[3, c] + total[8 * c : 8 * c + 8]
    for c in range(4):
        one, two = vh[1, 2 * c], vh[1, 2 * c + 1]
        edge[0, c] = jnp.where(row < 3, one, pltpu.roll(two, 3, 0))
        edge[1, c] = jnp.where(row < 3, pltpu.roll(one, 3, 0), two)
    send(edge.at[0], edge.at[3], sg.at[0], rg.at[0], (left, n))
    send(edge.at[1], edge.at[2], sg.at[1], rg.at[1], (right, n))
    forward_reacted(1, 0)

    wait(msfh.at[0], re.at[1])
    wait(msfh.at[0], re.at[2])
    wait(edge.at[3], rg.at[0])
    wait(edge.at[2], rg.at[1])
    for c in range(4):
        above, below = edge[2, c], edge[3, c]
        vh[0, 2 * c], vh[0, 2 * c + 1] = pltpu.roll(above, 5, 0), above
        vh[2, 2 * c], vh[2, 2 * c + 1] = below, pltpu.roll(below, 5, 0)

    def wide_rows(parts):
        return jnp.concatenate(
            [jnp.concatenate([part[c] for c in range(8)], axis=1) for part in parts], axis=0
        )

    rows24 = iota((24, 1024), 0)
    columns24 = iota((24, 1024), 1)
    outside = ((w == 0) & (rows24 < 8)) | ((w == wides - 1) & (rows24 >= 16))
    factor = wide_rows([msfh.at[0], ep.at[2], msfh.at[1]])
    vector = jnp.where(outside, 0.0, wide_rows([vh.at[0], vh.at[1], vh.at[2]]))
    vectors = [vector]
    for step in range(3):
        beside = pltpu.roll(vector, 1, 0) + pltpu.roll(vector, 23, 0)
        beside = beside + jnp.where(columns24 == 0, 0.0, pltpu.roll(vector, 1, 1))
        beside = beside + jnp.where(columns24 == 1023, 0.0, pltpu.roll(vector, 1023, 1))
        vector = jnp.where(outside, 0.0, ((4.0 - SHIFT) + factor) * vector - beside)
        vectors.append(vector)
    vectors = [v[8:16] for v in vectors]
    for k in range(3):
        for c in range(8):
            fields[k, c] = vectors[k][:, 128 * c : 128 * c + 128]
    sums = []
    for k in range(6):
        product = vectors[k // 2] * vectors[(k + 1) // 2]
        tile = product[:, :128]
        for c in range(1, 8):
            tile = tile + product[:, 128 * c : 128 * c + 128]
        sums.append(jnp.sum(tile, axis=0, keepdims=True))
    tile = jnp.concatenate(sums + [jnp.zeros((2, 128), F32)], axis=0)
    tile = jnp.sum(tile, axis=1, keepdims=True)
    diagonal = iota((8, 128), 0) == iota((8, 128), 1)
    mz[w] = jnp.sum(jnp.where(diagonal, tile, 0.0), axis=0, keepdims=True)
    for to in others:
        send(mz.at[w], mz.at[w], so.at[0], so.at[1], (to, n))

    wait_reacted(1, 0)
    diffuse(1, 0)
    amounts = pltpu.make_async_copy(diff.at[1], out_pops, loc.at[10])
    amounts.start()

    wait(mz.at[0 : wides - 1], so.at[1])
    tile = jnp.sum(mz[...].reshape(wides, 128), axis=0, keepdims=True)
    sums = jnp.sum(jnp.where(diagonal, tile, 0.0), axis=1, keepdims=True)
    a, b, c = krylov_coefficients([sums[k : k + 1] for k in range(6)])
    msf_v[...] = a * fields[0, n] + b * fields[1, n] + c * fields[2, n]
    voltage = pltpu.make_async_copy(msf_v, out_pot, loc.at[11])
    voltage.start()

    for k in range(2):
        wait(gath.at[k, 0:56], sa.at[k])
        wait(halo.at[k, 0:23], sh.at[k])
    wait(ep.at[:, 0:7], se.at[0])
    wait(msfh.at[0], se.at[1])
    wait(msfh.at[0], se.at[2])
    wait(uv.at[2:4, 0:56, :], su.at[0])
    wait(uv.at[0:2], su.at[1])
    wait(edge.at[0], sg.at[0])
    wait(edge.at[1], sg.at[1])
    wait(mz.at[0 : wides - 1], so.at[0])
    amounts.wait()
    voltage.wait()


def solution(mesh):
    zs = 8
    xs = mesh.shape["wide"] // zs

    def shards(pops, kinetic, sto, draws, rates, adjacency, tallies, coef, target, msf, prior):
        any_spec = pl.BlockSpec(memory_space=pl.ANY)
        hbm_spec = pl.BlockSpec(memory_space=pltpu.HBM)
        dma = pltpu.SemaphoreType.DMA
        vmem = pltpu.VMEM
        return pl.pallas_call(
            functools.partial(kernel, zs, xs),
            out_shape=(
                pltpu.VMEM(pops.shape, F32),
                pltpu.VMEM(msf.shape, F32),
            ),
            in_specs=[hbm_spec] * 11,
            out_specs=(any_spec, any_spec),
            scratch_shapes=[
                vmem((2, 64, 8, 128), F32),
                vmem((2, 64, 8, 128), F32),
                vmem((2, 24, 64, 128), F32),
                vmem((2, 8, 64, 128), F32),
                vmem((2, 8, 128, 128), jnp.int32),
                vmem((64, 128), F32),
                vmem((64, 128), F32),
                vmem((4, 64), jnp.int32),
                vmem((2, 4, 64), jnp.int32),
                vmem((64, 128), jnp.int32),
                vmem((8, 128), F32),
                vmem((8, 128), F32),
                pltpu.SMEM((8,), F32),
                pltpu.SMEM((8,), F32),
                vmem((4, 8, 8, 128), F32),
                vmem((2, 8, 8, 128), F32),
                vmem((128, 256), BF16),
                vmem((128, 256), BF16),
                vmem((2, 2, 64, 256), BF16),
                vmem((64, 128, 128), BF16),
                vmem((64, 64, 128), BF16),
                vmem((4, 64, 128), F32),
                vmem((3, 8, 8, 128), F32),
                vmem((4, 4, 8, 128), F32),
                vmem((3, 8, 8, 128), F32),
                vmem((zs * xs, 1, 128), F32),
                dma((12,)),
                dma((2,)),
                dma((2,)),
                dma((2,)),
                dma((2,)),
                dma((2, 4, 7)),
                dma((2, 4, 2, 8)),
                dma((3,)),
                dma((3,)),
                dma((2,)),
                dma((2,)),
                dma((2,)),
                dma((2,)),
                dma((2,)),
                pltpu.SemaphoreType.REGULAR((4,)),
            ],
            compiler_params=pltpu.CompilerParams(
                collective_id=0, has_side_effects=True, vmem_limit_bytes=VLIM * 1024 * 1024
            ),
        )(
            pops, kinetic.T, sto, draws, rates, adjacency.T, tallies.transpose(0, 2, 1), coef,
            target, msf, prior,
        )

    return jax.shard_map(
        shards,
        mesh=mesh,
        in_specs=(
            P("narrow", "wide", None),
            P(),
            P(),
            P(None, None, ("wide", "narrow"), None),
            P("narrow"),
            P("wide", None),
            P(None, "wide", None),
            P("narrow"),
            P("wide", None),
            P("wide", "narrow"),
            P("wide", "narrow"),
        ),
        out_specs=(P("narrow", "wide", None), P("wide", "narrow")),
        check_vma=False,
    )
```

```python
import functools

import jax
import jax.numpy as jnp
from jax import lax
from jax.experimental import pallas as pl
from jax.experimental.pallas import tpu as pltpu
from jax.sharding import PartitionSpec as P

MESH = pl.DeviceIdType.MESH
F32 = jnp.float32
BF16 = jnp.bfloat16

PARTNERS = ((1, 0), (3, 0), (1, 1), (3, 1), (2, 0), (2, 1), (0, 1))
FARTHEST = ((2, 1), (2, 0), (1, 1), (3, 1), (1, 0), (3, 0), (0, 1))
DIRECT = (((0, 1), (1, 0), (3, 1)), ((0, 1), (1, 0), (3, 0), (1, 1), (3, 1)))
SHIFT = 4.0
VLIM = 62
HALF = (4, 8)


def split(x):
    high = x.astype(BF16)
    return high, (x - high.astype(F32)).astype(BF16)


def dot(a, b):
    return jnp.dot(a, b, preferred_element_type=F32)


def dot_nt(a, b):
    return lax.dot_general(a, b, (((1,), (1,)), ((), ())), preferred_element_type=F32)


def iota(shape, dim):
    return lax.broadcasted_iota(jnp.int32, shape, dim)


def inner(p, q, moments):
    total = None
    for i, pi in enumerate(p):
        for j, qj in enumerate(q):
            term = pi * qj * moments[i + j]
            total = term if total is None else total + term
    return total


def krylov_coefficients(moments):
    one = jnp.ones_like(moments[0])
    direction, residual = [one], [one]
    x = [jnp.zeros_like(one)] * 3
    norm = moments[0]
    for iteration in range(3):
        size = len(direction)
        applied = [SHIFT * d for d in direction] + [jnp.zeros_like(one)]
        for i in range(size):
            applied[i + 1] = applied[i + 1] + direction[i]
        step = norm / inner(direction, applied, moments)
        x = [x[i] + step * direction[i] if i < size else x[i] for i in range(3)]
        if iteration == 2:
            return x
        residual = [
            (residual[i] if i < len(residual) else 0.0) - step * applied[i] for i in range(size + 1)
        ]
        fresh = inner(residual, residual, moments)
        ratio = fresh / norm
        norm = fresh
        direction = [
            residual[i] + ratio * direction[i] if i < size else residual[i] for i in range(size + 1)
        ]


def kernel(
    zs, xs,
    pops, kct, sto, draws, rates, adjt, talt, coef, tgt, msf, prior,
    out_pops, out_pot,
    gath, react, halo, diff, draws_v, kct_v, sto_v, adj_v, tal_v, tgt_v, msf_v, pri_v,
    rate_s, coef_s, ep, msfh, kmat, smat, wmat, lot, him, uv, vh, edge, fields, mz,
    loc, dloc, sa, ra, sh, r2, rh, se, re, su, ru, sg, rg, so, near,
):
    w, n = lax.axis_index("wide"), lax.axis_index("narrow")
    wides = zs * xs
    left, right = lax.rem(w + wides - 1, wides), lax.rem(w + 1, wides)
    y, core = n // 2, lax.rem(n, 2)
    x, z = w // zs, lax.rem(w, zs)

    def peer(rel):
        return lax.rem(y + rel[0], 4) * 2 + lax.rem(core + rel[1], 2)

    def source(rel):
        return peer(((4 - rel[0]) % 4, rel[1]))

    def eight(i):
        return pl.ds(pl.multiple_of(i * 8, 8), 8)

    def send(src, dst, s, r, to):
        pltpu.make_async_remote_copy(
            src_ref=src, dst_ref=dst, send_sem=s, recv_sem=r, device_id=to, device_id_type=MESH
        ).start()

    def wait(ref, sem):
        pltpu.make_async_copy(ref, ref, sem).wait()

    steps = [(i, j) for i in range(xs) for j in range(zs)][1:]
    steps.sort(key=lambda s: -(min(s[0], xs - s[0]) + min(s[1], zs - s[1])))
    others = [lax.rem(x + i, xs) * zs + lax.rem(z + j, zs) for i, j in steps]

    barrier = pltpu.get_barrier_semaphore()
    greet = [(w, peer(rel)) for rel in PARTNERS]
    greet += [(left, n), (right, n)]
    for to in greet:
        pl.semaphore_signal(barrier, inc=1, device_id=to, device_id_type=MESH)

    small = [
        (coef, coef_s), (rates, rate_s), (msf, msf_v), (prior, pri_v), (kct, kct_v), (sto, sto_v),
        (adjt, adj_v), (talt, tal_v), (tgt, tgt_v), (pops.at[:, eight(n), :], gath.at[0, eight(n)]),
    ]
    small = [pltpu.make_async_copy(s, d, loc.at[i]) for i, (s, d) in enumerate(small)]
    for copy in small:
        copy.start()
    for k in range(2):
        for b in range(8):
            pltpu.make_async_copy(draws.at[k, :, b, :], draws_v.at[k, b], dloc.at[k]).start()
    pl.semaphore_wait(barrier, len(greet))

    for rel in PARTNERS:
        m = peer(rel)
        send(pops.at[:, eight(m), :], gath.at[0, eight(n)], sa.at[0], ra.at[0], (w, m))


    def reach(level):
        far = 2**level
        for to in (lax.rem(w + far, wides), lax.rem(w + wides - far, wides)):
            pl.semaphore_signal(near.at[level], inc=1, device_id=(to, n), device_id_type=MESH)

    reach(0)

    for copy in small[:4]:
        copy.wait()
    row = iota((8, 128), 0)
    ca = jnp.zeros((8, 128), F32)
    cb = jnp.zeros((8, 128), F32)
    for i in range(8):
        ca = jnp.where(row == i, coef_s[i], ca)
        cb = jnp.where(row == i, rate_s[i], cb)
    ep[0, n] = ca
    ep[1, n] = ca * cb
    ep[2, n] = msf_v[...]
    ep[3, n] = msf_v[...] * pri_v[...]
    for rel in PARTNERS:
        send(ep.at[:, n], ep.at[:, n], se.at[0], re.at[0], (w, peer(rel)))

    for copy in small[4:9]:
        copy.wait()
    kt_high, kt_low = split(kct_v[...])
    kt = jnp.concatenate([kt_high, kt_low, kt_high, kt_low], axis=0).astype(F32)
    kmat[...] = kt.T.astype(BF16)
    s_high, s_low = split(sto_v[...])
    smat[...] = jnp.concatenate(
        [jnp.concatenate([s_high, s_high], 1), jnp.concatenate([s_low, s_low], 1)], axis=0
    )
    def tables(b, carry):
        node = tgt_v[pl.ds(b, 1), :]
        low = lax.rem(node, 128)
        high = lax.rem(node // 128, 8) * 8 + node // 1024
        lot[b] = jnp.where(iota((128, 128), 0) == low, 1.0, 0.0).astype(BF16)
        him[b] = jnp.where(iota((64, 128), 0) == high, 1.0, 0.0).astype(BF16)
        return carry

    def hop_tables():
        place = iota((256, 128), 0)
        own = iota((256, 128), 1)
        inside = jnp.where(place >= 128, place - 128, place)
        inside = jnp.where(inside >= 64, inside - 64, inside)
        for k in range(2):
            for part in range(2):
                if part == 0:
                    named = inside + jnp.where(place < 128, 64, 0)
                else:
                    named = inside + 128
                table = jnp.zeros((256, 128), F32)
                for j in range(4):
                    pad = jnp.zeros((1, 64), jnp.int32)
                    near = jnp.concatenate([adj_v[j : j + 1, :] - (w * 64 - 64), pad], axis=1)
                    tally = jnp.concatenate([tal_v[k, j : j + 1, :], pad], axis=1)
                    weight = tally.astype(F32) * 0.5
                    table = table + jnp.where(named == near, weight, 0.0)
                    if part == 0:
                        table = table - jnp.where(named == own + 64, weight, 0.0)
                wmat[k, part] = table.T[:64].astype(BF16)


    def chemistry(k):
        wait(draws_v.at[k], dloc.at[k])
        populations = gath.at[k].reshape(512, 128)
        reacted = react.at[k].reshape(512, 128)
        for pair in range(4):
            blocks = (2 * pair, 2 * pair + 1)
            p = jnp.concatenate([populations[pl.ds(b, 64, stride=8), :] for b in blocks], axis=1)
            high, low = split(p)
            propensity = dot(kmat[...], jnp.concatenate([high, high, low, low], axis=0))
            d = jnp.concatenate([draws_v[k, b] for b in blocks], axis=1)
            fired = propensity * (d.astype(F32) * (1.0 / 3.5))
            change = dot(smat[...], jnp.concatenate(split(fired), axis=0))
            p = p + 0.25 * (change[:64] + change[64:])
            for i, b in enumerate(blocks):
                reacted[pl.ds(b, 64, stride=8), :] = p[:, 128 * i : 128 * i + 128]

    def chunk(k, side, m, h):
        return halo.at[k, pl.ds(8 * side + HALF[k] * h, HALF[k]), eight(m), :]

    def send_reacted(k, h):
        def reacted(m):
            return react.at[k, pl.ds(pl.multiple_of(8 * m + HALF[k] * h, HALF[k]), HALF[k])]

        for i, rel in enumerate(PARTNERS):
            m = peer(rel)
            send(reacted(m), chunk(k, 1, n, h), sh.at[k], r2.at[k, h, i], (w, m))
        for rel in ((0, 0),) + DIRECT[k]:
            m = peer(rel)
            slot = 7 if rel == (0, 0) else PARTNERS.index(rel)
            send(reacted(m), chunk(k, 2, n, h), sh.at[k], rh.at[k, h, 1, slot], (left, m))
            send(reacted(m), chunk(k, 0, n, h), sh.at[k], rh.at[k, h, 0, slot], (right, m))

    def keep_reacted(k):
        halo[k, 8:16, eight(n), :] = react[k, eight(n)]

    def forward_reacted(k, h):
        for i, rel in enumerate(PARTNERS):
            if rel in DIRECT[k]:
                continue
            m = source(rel)
            wait(chunk(k, 1, m, h), r2.at[k, h, i])
            send(chunk(k, 1, m, h), chunk(k, 2, m, h), sh.at[k], rh.at[k, h, 1, i], (left, n))
            send(chunk(k, 1, m, h), chunk(k, 0, m, h), sh.at[k], rh.at[k, h, 0, i], (right, n))

    def wait_reacted(k, h):
        for i, rel in enumerate(PARTNERS):
            if rel in DIRECT[k]:
                wait(chunk(k, 1, source(rel), h), r2.at[k, h, i])
        for i, rel in enumerate(PARTNERS + ((0, 0),)):
            for side in (0, 1):
                wait(chunk(k, 2 * side, source(rel), h), rh.at[k, h, side, i])

    def diffuse(k, h):
        for pair in range(HALF[k] // 2 * h, HALF[k] // 2 * (h + 1)):
            parts = [
                split(
                    jnp.concatenate(
                        [halo[k, 8 * side + 2 * pair + i] for i in range(2)], axis=1
                    )
                )
                for side in (1, 0, 2)
            ]
            first = jnp.concatenate(parts[0] + parts[1], axis=0)
            second = jnp.concatenate(parts[2], axis=0)
            flux = dot(wmat[k, 0], first) + dot(wmat[k, 1, :, :128], second)
            for i in range(2):
                s = 2 * pair + i
                diff[k, s] = halo[k, 8 + s] + rate_s[s] * flux[:, 128 * i : 128 * i + 128]

    wait(gath.at[0, 0:56], ra.at[0])
    small[9].wait()
    chemistry(0)
    pl.semaphore_wait(near.at[0], 2)
    reach(1)
    for h in range(8 // HALF[0]):
        send_reacted(0, h)
    keep_reacted(0)
    forward_reacted(0, 0)
    hop_tables()
    forward_reacted(0, 1)
    pl.semaphore_wait(near.at[1], 2)
    reach(2)
    lax.fori_loop(0, 24, tables, 0)
    for h in range(8 // HALF[0]):
        wait_reacted(0, h)
        diffuse(0, h)
        for rel in PARTNERS:
            m = peer(rel)
            send(
                diff.at[0, pl.ds(HALF[0] * h, HALF[0]), eight(m), :],
                gath.at[1, pl.ds(pl.multiple_of(8 * n + HALF[0] * h, HALF[0]), HALF[0])],
                sa.at[1], ra.at[1], (w, m),
            )
    gath[1, eight(n)] = diff[0, :, eight(n), :]
    pl.semaphore_wait(near.at[2], 2)
    reach(3)
    lax.fori_loop(24, 64, tables, 0)
    wait(ep.at[:, 0:7], re.at[0])
    send(ep.at[2], msfh.at[1], se.at[1], re.at[1], (left, n))
    send(ep.at[2], msfh.at[0], se.at[2], re.at[2], (right, n))


    wait(gath.at[1, 0:56], ra.at[1])
    chemistry(1)
    u = jnp.zeros((8, 128), F32)
    v = jnp.zeros((8, 128), F32)
    for s in range(64):
        tile = react[1, s]
        u = u + ep[0, s // 8, s % 8 : s % 8 + 1, :] * tile
        v = v + ep[1, s // 8, s % 8 : s % 8 + 1, :] * tile
    uv[2, eight(n)] = v
    uv[3, eight(n)] = u
    for rel in FARTHEST + ((0, 0),):
        send(uv.at[2, eight(n)], uv.at[1, eight(n)], su.at[1], ru.at[1], (left, peer(rel)))
        send(uv.at[2, eight(n)], uv.at[0, eight(n)], su.at[1], ru.at[1], (right, peer(rel)))
    for rel in FARTHEST:
        mine = uv.at[2:4, eight(n), :]
        send(mine, mine, su.at[0], ru.at[0], (w, peer(rel)))
    send_reacted(1, 0)
    keep_reacted(1)
    pl.semaphore_wait(near.at[3], 2)

    wait(uv.at[2:4, 0:56, :], ru.at[0])
    wait(uv.at[0:2], ru.at[1])
    vs, vl, vr = split(uv[2]), split(uv[0]), split(uv[1])
    current = (
        uv[3]
        + dot(wmat[1, 0], jnp.concatenate(vs + vl, axis=0))
        + dot(wmat[1, 1, :, :128], jnp.concatenate(vr, axis=0))
    )
    c_high, c_low = split(current)
    total = jnp.zeros((128, 128), F32)
    for pair in range(32):
        rows, columns = [], []
        for b in (2 * pair, 2 * pair + 1):
            mask = him[b]
            rows.append(
                jnp.concatenate([mask * c_high[b : b + 1], mask * c_low[b : b + 1]], axis=0)
            )
            columns.append(lot[b])
        total = total + dot_nt(jnp.concatenate(rows, axis=1), jnp.concatenate(columns, axis=1))
    total = total[:64] + total[64:]
    for c in range(8):
        vh[1, c] = ep[3, c] + total[8 * c : 8 * c + 8]
    for c in range(4):
        one, two = vh[1, 2 * c], vh[1, 2 * c + 1]
        edge[0, c] = jnp.where(row < 3, one, pltpu.roll(two, 3, 0))
        edge[1, c] = jnp.where(row < 3, pltpu.roll(one, 3, 0), two)
    send(edge.at[0], edge.at[3], sg.at[0], rg.at[0], (left, n))
    send(edge.at[1], edge.at[2], sg.at[1], rg.at[1], (right, n))
    forward_reacted(1, 0)

    wait(msfh.at[0], re.at[1])
    wait(msfh.at[0], re.at[2])
    wait(edge.at[3], rg.at[0])
    wait(edge.at[2], rg.at[1])
    for c in range(4):
        above, below = edge[2, c], edge[3, c]
        vh[0, 2 * c], vh[0, 2 * c + 1] = pltpu.roll(above, 5, 0), above
        vh[2, 2 * c], vh[2, 2 * c + 1] = below, pltpu.roll(below, 5, 0)

    def wide_rows(parts):
        return jnp.concatenate(
            [jnp.concatenate([part[c] for c in range(8)], axis=1) for part in parts], axis=0
        )

    rows24 = iota((24, 1024), 0)
    columns24 = iota((24, 1024), 1)
    outside = ((w == 0) & (rows24 < 8)) | ((w == wides - 1) & (rows24 >= 16))
    factor = wide_rows([msfh.at[0], ep.at[2], msfh.at[1]])
    vector = jnp.where(outside, 0.0, wide_rows([vh.at[0], vh.at[1], vh.at[2]]))
    vectors = [vector]
    for step in range(3):
        beside = pltpu.roll(vector, 1, 0) + pltpu.roll(vector, 23, 0)
        beside = beside + jnp.where(columns24 == 0, 0.0, pltpu.roll(vector, 1, 1))
        beside = beside + jnp.where(columns24 == 1023, 0.0, pltpu.roll(vector, 1023, 1))
        vector = jnp.where(outside, 0.0, ((4.0 - SHIFT) + factor) * vector - beside)
        vectors.append(vector)
    vectors = [v[8:16] for v in vectors]
    for k in range(3):
        for c in range(8):
            fields[k, c] = vectors[k][:, 128 * c : 128 * c + 128]
    sums = []
    for k in range(6):
        product = vectors[k // 2] * vectors[(k + 1) // 2]
        tile = product[:, :128]
        for c in range(1, 8):
            tile = tile + product[:, 128 * c : 128 * c + 128]
        sums.append(jnp.sum(tile, axis=0, keepdims=True))
    tile = jnp.concatenate(sums + [jnp.zeros((2, 128), F32)], axis=0)
    tile = jnp.sum(tile, axis=1, keepdims=True)
    diagonal = iota((8, 128), 0) == iota((8, 128), 1)
    mz[w] = jnp.sum(jnp.where(diagonal, tile, 0.0), axis=0, keepdims=True)
    for to in others:
        send(mz.at[w], mz.at[w], so.at[0], so.at[1], (to, n))

    wait_reacted(1, 0)
    diffuse(1, 0)
    amounts = pltpu.make_async_copy(diff.at[1], out_pops, loc.at[10])
    amounts.start()

    wait(mz.at[0 : wides - 1], so.at[1])
    tile = jnp.sum(mz[...].reshape(wides, 128), axis=0, keepdims=True)
    sums = jnp.sum(jnp.where(diagonal, tile, 0.0), axis=1, keepdims=True)
    a, b, c = krylov_coefficients([sums[k : k + 1] for k in range(6)])
    msf_v[...] = a * fields[0, n] + b * fields[1, n] + c * fields[2, n]
    voltage = pltpu.make_async_copy(msf_v, out_pot, loc.at[11])
    voltage.start()

    for k in range(2):
        wait(gath.at[k, 0:56], sa.at[k])
        wait(halo.at[k, 0:23], sh.at[k])
    wait(ep.at[:, 0:7], se.at[0])
    wait(msfh.at[0], se.at[1])
    wait(msfh.at[0], se.at[2])
    wait(uv.at[2:4, 0:56, :], su.at[0])
    wait(uv.at[0:2], su.at[1])
    wait(edge.at[0], sg.at[0])
    wait(edge.at[1], sg.at[1])
    wait(mz.at[0 : wides - 1], so.at[0])
    amounts.wait()
    voltage.wait()


def solution(mesh):
    zs = 8
    xs = mesh.shape["wide"] // zs

    def shards(pops, kinetic, sto, draws, rates, adjacency, tallies, coef, target, msf, prior):
        any_spec = pl.BlockSpec(memory_space=pl.ANY)
        hbm_spec = pl.BlockSpec(memory_space=pltpu.HBM)
        dma = pltpu.SemaphoreType.DMA
        vmem = pltpu.VMEM
        return pl.pallas_call(
            functools.partial(kernel, zs, xs),
            out_shape=(
                pltpu.VMEM(pops.shape, F32),
                pltpu.VMEM(msf.shape, F32),
            ),
            in_specs=[hbm_spec] * 11,
            out_specs=(any_spec, any_spec),
            scratch_shapes=[
                vmem((2, 64, 8, 128), F32),
                vmem((2, 64, 8, 128), F32),
                vmem((2, 24, 64, 128), F32),
                vmem((2, 8, 64, 128), F32),
                vmem((2, 8, 128, 128), jnp.int32),
                vmem((64, 128), F32),
                vmem((64, 128), F32),
                vmem((4, 64), jnp.int32),
                vmem((2, 4, 64), jnp.int32),
                vmem((64, 128), jnp.int32),
                vmem((8, 128), F32),
                vmem((8, 128), F32),
                pltpu.SMEM((8,), F32),
                pltpu.SMEM((8,), F32),
                vmem((4, 8, 8, 128), F32),
                vmem((2, 8, 8, 128), F32),
                vmem((128, 256), BF16),
                vmem((128, 256), BF16),
                vmem((2, 2, 64, 256), BF16),
                vmem((64, 128, 128), BF16),
                vmem((64, 64, 128), BF16),
                vmem((4, 64, 128), F32),
                vmem((3, 8, 8, 128), F32),
                vmem((4, 4, 8, 128), F32),
                vmem((3, 8, 8, 128), F32),
                vmem((zs * xs, 1, 128), F32),
                dma((12,)),
                dma((2,)),
                dma((2,)),
                dma((2,)),
                dma((2,)),
                dma((2, 4, 7)),
                dma((2, 4, 2, 8)),
                dma((3,)),
                dma((3,)),
                dma((2,)),
                dma((2,)),
                dma((2,)),
                dma((2,)),
                dma((2,)),
                pltpu.SemaphoreType.REGULAR((4,)),
            ],
            compiler_params=pltpu.CompilerParams(
                collective_id=0, has_side_effects=True, vmem_limit_bytes=VLIM * 1024 * 1024
            ),
        )(
            pops, kinetic.T, sto, draws, rates, adjacency.T, tallies.transpose(0, 2, 1), coef,
            target, msf, prior,
        )

    return jax.shard_map(
        shards,
        mesh=mesh,
        in_specs=(
            P("narrow", "wide", None),
            P(),
            P(),
            P(None, None, ("wide", "narrow"), None),
            P("narrow"),
            P("wide", None),
            P(None, "wide", None),
            P("narrow"),
            P("wide", None),
            P("wide", "narrow"),
            P("wide", "narrow"),
        ),
        out_specs=(P("narrow", "wide", None), P("wide", "narrow")),
        check_vma=False,
    )
```

```python
import functools

import jax
import jax.numpy as jnp
from jax import lax
from jax.experimental import pallas as pl
from jax.experimental.pallas import tpu as pltpu
from jax.sharding import PartitionSpec as P

MESH = pl.DeviceIdType.MESH
F32 = jnp.float32
BF16 = jnp.bfloat16

PARTNERS = ((1, 0), (3, 0), (1, 1), (3, 1), (2, 0), (2, 1), (0, 1))
FARTHEST = ((2, 1), (2, 0), (1, 1), (3, 1), (1, 0), (3, 0), (0, 1))
DIRECT = (((0, 1), (1, 0), (3, 1)), ((0, 1), (1, 0), (3, 0), (1, 1), (3, 1)))
SHIFT = 4.0
VLIM = 62
HALF = (2, 8)


def split(x):
    high = x.astype(BF16)
    return high, (x - high.astype(F32)).astype(BF16)


def dot(a, b):
    return jnp.dot(a, b, preferred_element_type=F32)


def dot_nt(a, b):
    return lax.dot_general(a, b, (((1,), (1,)), ((), ())), preferred_element_type=F32)


def iota(shape, dim):
    return lax.broadcasted_iota(jnp.int32, shape, dim)


def inner(p, q, moments):
    total = None
    for i, pi in enumerate(p):
        for j, qj in enumerate(q):
            term = pi * qj * moments[i + j]
            total = term if total is None else total + term
    return total


def krylov_coefficients(moments):
    one = jnp.ones_like(moments[0])
    direction, residual = [one], [one]
    x = [jnp.zeros_like(one)] * 3
    norm = moments[0]
    for iteration in range(3):
        size = len(direction)
        applied = [SHIFT * d for d in direction] + [jnp.zeros_like(one)]
        for i in range(size):
            applied[i + 1] = applied[i + 1] + direction[i]
        step = norm / inner(direction, applied, moments)
        x = [x[i] + step * direction[i] if i < size else x[i] for i in range(3)]
        if iteration == 2:
            return x
        residual = [
            (residual[i] if i < len(residual) else 0.0) - step * applied[i] for i in range(size + 1)
        ]
        fresh = inner(residual, residual, moments)
        ratio = fresh / norm
        norm = fresh
        direction = [
            residual[i] + ratio * direction[i] if i < size else residual[i] for i in range(size + 1)
        ]


def kernel(
    zs, xs,
    pops, kct, sto, draws, rates, adjt, talt, coef, tgt, msf, prior,
    out_pops, out_pot,
    gath, react, halo, diff, draws_v, kct_v, sto_v, adj_v, tal_v, tgt_v, msf_v, pri_v,
    rate_s, coef_s, ep, msfh, kmat, smat, wmat, lot, him, uv, vh, edge, fields, mz,
    loc, dloc, sa, ra, sh, r2, rh, se, re, su, ru, sg, rg, so, near,
):
    w, n = lax.axis_index("wide"), lax.axis_index("narrow")
    wides = zs * xs
    left, right = lax.rem(w + wides - 1, wides), lax.rem(w + 1, wides)
    y, core = n // 2, lax.rem(n, 2)
    x, z = w // zs, lax.rem(w, zs)

    def peer(rel):
        return lax.rem(y + rel[0], 4) * 2 + lax.rem(core + rel[1], 2)

    def source(rel):
        return peer(((4 - rel[0]) % 4, rel[1]))

    def eight(i):
        return pl.ds(pl.multiple_of(i * 8, 8), 8)

    def send(src, dst, s, r, to):
        pltpu.make_async_remote_copy(
            src_ref=src, dst_ref=dst, send_sem=s, recv_sem=r, device_id=to, device_id_type=MESH
        ).start()

    def wait(ref, sem):
        pltpu.make_async_copy(ref, ref, sem).wait()

    steps = [(i, j) for i in range(xs) for j in range(zs)][1:]
    steps.sort(key=lambda s: -(min(s[0], xs - s[0]) + min(s[1], zs - s[1])))
    others = [lax.rem(x + i, xs) * zs + lax.rem(z + j, zs) for i, j in steps]

    barrier = pltpu.get_barrier_semaphore()
    greet = [(w, peer(rel)) for rel in PARTNERS]
    greet += [(left, n), (right, n)]
    for to in greet:
        pl.semaphore_signal(barrier, inc=1, device_id=to, device_id_type=MESH)

    small = [
        (coef, coef_s), (rates, rate_s), (msf, msf_v), (prior, pri_v), (kct, kct_v), (sto, sto_v),
        (adjt, adj_v), (talt, tal_v), (tgt, tgt_v), (pops.at[:, eight(n), :], gath.at[0, eight(n)]),
    ]
    small = [pltpu.make_async_copy(s, d, loc.at[i]) for i, (s, d) in enumerate(small)]
    for copy in small:
        copy.start()
    for k in range(2):
        for b in range(8):
            pltpu.make_async_copy(draws.at[k, :, b, :], draws_v.at[k, b], dloc.at[k]).start()
    pl.semaphore_wait(barrier, len(greet))

    for rel in PARTNERS:
        m = peer(rel)
        send(pops.at[:, eight(m), :], gath.at[0, eight(n)], sa.at[0], ra.at[0], (w, m))


    def reach(level):
        far = 2**level
        for to in (lax.rem(w + far, wides), lax.rem(w + wides - far, wides)):
            pl.semaphore_signal(near.at[level], inc=1, device_id=(to, n), device_id_type=MESH)

    reach(0)

    for copy in small[:4]:
        copy.wait()
    row = iota((8, 128), 0)
    ca = jnp.zeros((8, 128), F32)
    cb = jnp.zeros((8, 128), F32)
    for i in range(8):
        ca = jnp.where(row == i, coef_s[i], ca)
        cb = jnp.where(row == i, rate_s[i], cb)
    ep[0, n] = ca
    ep[1, n] = ca * cb
    ep[2, n] = msf_v[...]
    ep[3, n] = msf_v[...] * pri_v[...]
    for rel in PARTNERS:
        send(ep.at[:, n], ep.at[:, n], se.at[0], re.at[0], (w, peer(rel)))

    for copy in small[4:9]:
        copy.wait()
    kt_high, kt_low = split(kct_v[...])
    kt = jnp.concatenate([kt_high, kt_low, kt_high, kt_low], axis=0).astype(F32)
    kmat[...] = kt.T.astype(BF16)
    s_high, s_low = split(sto_v[...])
    smat[...] = jnp.concatenate(
        [jnp.concatenate([s_high, s_high], 1), jnp.concatenate([s_low, s_low], 1)], axis=0
    )
    def tables(b, carry):
        node = tgt_v[pl.ds(b, 1), :]
        low = lax.rem(node, 128)
        high = lax.rem(node // 128, 8) * 8 + node // 1024
        lot[b] = jnp.where(iota((128, 128), 0) == low, 1.0, 0.0).astype(BF16)
        him[b] = jnp.where(iota((64, 128), 0) == high, 1.0, 0.0).astype(BF16)
        return carry

    def hop_tables():
        place = iota((256, 128), 0)
        own = iota((256, 128), 1)
        inside = jnp.where(place >= 128, place - 128, place)
        inside = jnp.where(inside >= 64, inside - 64, inside)
        for k in range(2):
            for part in range(2):
                if part == 0:
                    named = inside + jnp.where(place < 128, 64, 0)
                else:
                    named = inside + 128
                table = jnp.zeros((256, 128), F32)
                for j in range(4):
                    pad = jnp.zeros((1, 64), jnp.int32)
                    near = jnp.concatenate([adj_v[j : j + 1, :] - (w * 64 - 64), pad], axis=1)
                    tally = jnp.concatenate([tal_v[k, j : j + 1, :], pad], axis=1)
                    weight = tally.astype(F32) * 0.5
                    table = table + jnp.where(named == near, weight, 0.0)
                    if part == 0:
                        table = table - jnp.where(named == own + 64, weight, 0.0)
                wmat[k, part] = table.T[:64].astype(BF16)


    def chemistry(k):
        wait(draws_v.at[k], dloc.at[k])
        populations = gath.at[k].reshape(512, 128)
        reacted = react.at[k].reshape(512, 128)
        for pair in range(4):
            blocks = (2 * pair, 2 * pair + 1)
            p = jnp.concatenate([populations[pl.ds(b, 64, stride=8), :] for b in blocks], axis=1)
            high, low = split(p)
            propensity = dot(kmat[...], jnp.concatenate([high, high, low, low], axis=0))
            d = jnp.concatenate([draws_v[k, b] for b in blocks], axis=1)
            fired = propensity * (d.astype(F32) * (1.0 / 3.5))
            change = dot(smat[...], jnp.concatenate(split(fired), axis=0))
            p = p + 0.25 * (change[:64] + change[64:])
            for i, b in enumerate(blocks):
                reacted[pl.ds(b, 64, stride=8), :] = p[:, 128 * i : 128 * i + 128]

    def chunk(k, side, m, h):
        return halo.at[k, pl.ds(8 * side + HALF[k] * h, HALF[k]), eight(m), :]

    def send_reacted(k, h):
        def reacted(m):
            return react.at[k, pl.ds(pl.multiple_of(8 * m + HALF[k] * h, HALF[k]), HALF[k])]

        for i, rel in enumerate(PARTNERS):
            m = peer(rel)
            send(reacted(m), chunk(k, 1, n, h), sh.at[k], r2.at[k, h, i], (w, m))
        for rel in ((0, 0),) + DIRECT[k]:
            m = peer(rel)
            slot = 7 if rel == (0, 0) else PARTNERS.index(rel)
            send(reacted(m), chunk(k, 2, n, h), sh.at[k], rh.at[k, h, 1, slot], (left, m))
            send(reacted(m), chunk(k, 0, n, h), sh.at[k], rh.at[k, h, 0, slot], (right, m))

    def keep_reacted(k):
        halo[k, 8:16, eight(n), :] = react[k, eight(n)]

    def forward_reacted(k, h):
        for i, rel in enumerate(PARTNERS):
            if rel in DIRECT[k]:
                continue
            m = source(rel)
            wait(chunk(k, 1, m, h), r2.at[k, h, i])
            send(chunk(k, 1, m, h), chunk(k, 2, m, h), sh.at[k], rh.at[k, h, 1, i], (left, n))
            send(chunk(k, 1, m, h), chunk(k, 0, m, h), sh.at[k], rh.at[k, h, 0, i], (right, n))

    def wait_reacted(k, h):
        for i, rel in enumerate(PARTNERS):
            if rel in DIRECT[k]:
                wait(chunk(k, 1, source(rel), h), r2.at[k, h, i])
        for i, rel in enumerate(PARTNERS + ((0, 0),)):
            for side in (0, 1):
                wait(chunk(k, 2 * side, source(rel), h), rh.at[k, h, side, i])

    def diffuse(k, h):
        for pair in range(HALF[k] // 2 * h, HALF[k] // 2 * (h + 1)):
            parts = [
                split(
                    jnp.concatenate(
                        [halo[k, 8 * side + 2 * pair + i] for i in range(2)], axis=1
                    )
                )
                for side in (1, 0, 2)
            ]
            first = jnp.concatenate(parts[0] + parts[1], axis=0)
            second = jnp.concatenate(parts[2], axis=0)
            flux = dot(wmat[k, 0], first) + dot(wmat[k, 1, :, :128], second)
            for i in range(2):
                s = 2 * pair + i
                diff[k, s] = halo[k, 8 + s] + rate_s[s] * flux[:, 128 * i : 128 * i + 128]

    wait(gath.at[0, 0:56], ra.at[0])
    small[9].wait()
    chemistry(0)
    pl.semaphore_wait(near.at[0], 2)
    reach(1)
    for h in range(8 // HALF[0]):
        send_reacted(0, h)
    keep_reacted(0)
    forward_reacted(0, 0)
    forward_reacted(0, 1)
    hop_tables()
    forward_reacted(0, 2)
    forward_reacted(0, 3)
    pl.semaphore_wait(near.at[1], 2)
    reach(2)
    lax.fori_loop(0, 24, tables, 0)
    for h in range(8 // HALF[0]):
        wait_reacted(0, h)
        diffuse(0, h)
        for rel in PARTNERS:
            m = peer(rel)
            send(
                diff.at[0, pl.ds(HALF[0] * h, HALF[0]), eight(m), :],
                gath.at[1, pl.ds(pl.multiple_of(8 * n + HALF[0] * h, HALF[0]), HALF[0])],
                sa.at[1], ra.at[1], (w, m),
            )
    gath[1, eight(n)] = diff[0, :, eight(n), :]
    pl.semaphore_wait(near.at[2], 2)
    reach(3)
    lax.fori_loop(24, 64, tables, 0)
    wait(ep.at[:, 0:7], re.at[0])
    send(ep.at[2], msfh.at[1], se.at[1], re.at[1], (left, n))
    send(ep.at[2], msfh.at[0], se.at[2], re.at[2], (right, n))


    wait(gath.at[1, 0:56], ra.at[1])
    chemistry(1)
    u = jnp.zeros((8, 128), F32)
    v = jnp.zeros((8, 128), F32)
    for s in range(64):
        tile = react[1, s]
        u = u + ep[0, s // 8, s % 8 : s % 8 + 1, :] * tile
        v = v + ep[1, s // 8, s % 8 : s % 8 + 1, :] * tile
    uv[2, eight(n)] = v
    uv[3, eight(n)] = u
    for rel in FARTHEST + ((0, 0),):
        send(uv.at[2, eight(n)], uv.at[1, eight(n)], su.at[1], ru.at[1], (left, peer(rel)))
        send(uv.at[2, eight(n)], uv.at[0, eight(n)], su.at[1], ru.at[1], (right, peer(rel)))
    for rel in FARTHEST:
        mine = uv.at[2:4, eight(n), :]
        send(mine, mine, su.at[0], ru.at[0], (w, peer(rel)))
    send_reacted(1, 0)
    keep_reacted(1)
    pl.semaphore_wait(near.at[3], 2)

    wait(uv.at[2:4, 0:56, :], ru.at[0])
    wait(uv.at[0:2], ru.at[1])
    vs, vl, vr = split(uv[2]), split(uv[0]), split(uv[1])
    current = (
        uv[3]
        + dot(wmat[1, 0], jnp.concatenate(vs + vl, axis=0))
        + dot(wmat[1, 1, :, :128], jnp.concatenate(vr, axis=0))
    )
    c_high, c_low = split(current)
    total = jnp.zeros((128, 128), F32)
    for pair in range(32):
        rows, columns = [], []
        for b in (2 * pair, 2 * pair + 1):
            mask = him[b]
            rows.append(
                jnp.concatenate([mask * c_high[b : b + 1], mask * c_low[b : b + 1]], axis=0)
            )
            columns.append(lot[b])
        total = total + dot_nt(jnp.concatenate(rows, axis=1), jnp.concatenate(columns, axis=1))
    total = total[:64] + total[64:]
    for c in range(8):
        vh[1, c] = ep[3, c] + total[8 * c : 8 * c + 8]
    for c in range(4):
        one, two = vh[1, 2 * c], vh[1, 2 * c + 1]
        edge[0, c] = jnp.where(row < 3, one, pltpu.roll(two, 3, 0))
        edge[1, c] = jnp.where(row < 3, pltpu.roll(one, 3, 0), two)
    send(edge.at[0], edge.at[3], sg.at[0], rg.at[0], (left, n))
    send(edge.at[1], edge.at[2], sg.at[1], rg.at[1], (right, n))
    forward_reacted(1, 0)

    wait(msfh.at[0], re.at[1])
    wait(msfh.at[0], re.at[2])
    wait(edge.at[3], rg.at[0])
    wait(edge.at[2], rg.at[1])
    for c in range(4):
        above, below = edge[2, c], edge[3, c]
        vh[0, 2 * c], vh[0, 2 * c + 1] = pltpu.roll(above, 5, 0), above
        vh[2, 2 * c], vh[2, 2 * c + 1] = below, pltpu.roll(below, 5, 0)

    def wide_rows(parts):
        return jnp.concatenate(
            [jnp.concatenate([part[c] for c in range(8)], axis=1) for part in parts], axis=0
        )

    rows24 = iota((24, 1024), 0)
    columns24 = iota((24, 1024), 1)
    outside = ((w == 0) & (rows24 < 8)) | ((w == wides - 1) & (rows24 >= 16))
    factor = wide_rows([msfh.at[0], ep.at[2], msfh.at[1]])
    vector = jnp.where(outside, 0.0, wide_rows([vh.at[0], vh.at[1], vh.at[2]]))
    vectors = [vector]
    for step in range(3):
        beside = pltpu.roll(vector, 1, 0) + pltpu.roll(vector, 23, 0)
        beside = beside + jnp.where(columns24 == 0, 0.0, pltpu.roll(vector, 1, 1))
        beside = beside + jnp.where(columns24 == 1023, 0.0, pltpu.roll(vector, 1023, 1))
        vector = jnp.where(outside, 0.0, ((4.0 - SHIFT) + factor) * vector - beside)
        vectors.append(vector)
    vectors = [v[8:16] for v in vectors]
    for k in range(3):
        for c in range(8):
            fields[k, c] = vectors[k][:, 128 * c : 128 * c + 128]
    sums = []
    for k in range(6):
        product = vectors[k // 2] * vectors[(k + 1) // 2]
        tile = product[:, :128]
        for c in range(1, 8):
            tile = tile + product[:, 128 * c : 128 * c + 128]
        sums.append(jnp.sum(tile, axis=0, keepdims=True))
    tile = jnp.concatenate(sums + [jnp.zeros((2, 128), F32)], axis=0)
    tile = jnp.sum(tile, axis=1, keepdims=True)
    diagonal = iota((8, 128), 0) == iota((8, 128), 1)
    mz[w] = jnp.sum(jnp.where(diagonal, tile, 0.0), axis=0, keepdims=True)
    for to in others:
        send(mz.at[w], mz.at[w], so.at[0], so.at[1], (to, n))

    wait_reacted(1, 0)
    diffuse(1, 0)
    amounts = pltpu.make_async_copy(diff.at[1], out_pops, loc.at[10])
    amounts.start()

    for k in range(2):
        wait(gath.at[k, 0:56], sa.at[k])
        wait(halo.at[k, 0:23], sh.at[k])
    wait(ep.at[:, 0:7], se.at[0])
    wait(msfh.at[0], se.at[1])
    wait(msfh.at[0], se.at[2])
    wait(uv.at[2:4, 0:56, :], su.at[0])
    wait(uv.at[0:2], su.at[1])
    wait(edge.at[0], sg.at[0])
    wait(edge.at[1], sg.at[1])
    wait(mz.at[0 : wides - 1], so.at[1])
    tile = jnp.sum(mz[...].reshape(wides, 128), axis=0, keepdims=True)
    sums = jnp.sum(jnp.where(diagonal, tile, 0.0), axis=1, keepdims=True)
    a, b, c = krylov_coefficients([sums[k : k + 1] for k in range(6)])
    out_pot[...] = a * fields[0, n] + b * fields[1, n] + c * fields[2, n]

    wait(mz.at[0 : wides - 1], so.at[0])
    amounts.wait()


def solution(mesh):
    zs = 8
    xs = mesh.shape["wide"] // zs

    def shards(pops, kinetic, sto, draws, rates, adjacency, tallies, coef, target, msf, prior):
        any_spec = pl.BlockSpec(memory_space=pl.ANY)
        hbm_spec = pl.BlockSpec(memory_space=pltpu.HBM)
        dma = pltpu.SemaphoreType.DMA
        vmem = pltpu.VMEM
        return pl.pallas_call(
            functools.partial(kernel, zs, xs),
            out_shape=(
                pltpu.VMEM(pops.shape, F32),
                pltpu.VMEM(msf.shape, F32),
            ),
            in_specs=[hbm_spec] * 11,
            out_specs=(any_spec, pl.BlockSpec(memory_space=pltpu.VMEM)),
            scratch_shapes=[
                vmem((2, 64, 8, 128), F32),
                vmem((2, 64, 8, 128), F32),
                vmem((2, 24, 64, 128), F32),
                vmem((2, 8, 64, 128), F32),
                vmem((2, 8, 128, 128), jnp.int32),
                vmem((64, 128), F32),
                vmem((64, 128), F32),
                vmem((4, 64), jnp.int32),
                vmem((2, 4, 64), jnp.int32),
                vmem((64, 128), jnp.int32),
                vmem((8, 128), F32),
                vmem((8, 128), F32),
                pltpu.SMEM((8,), F32),
                pltpu.SMEM((8,), F32),
                vmem((4, 8, 8, 128), F32),
                vmem((2, 8, 8, 128), F32),
                vmem((128, 256), BF16),
                vmem((128, 256), BF16),
                vmem((2, 2, 64, 256), BF16),
                vmem((64, 128, 128), BF16),
                vmem((64, 64, 128), BF16),
                vmem((4, 64, 128), F32),
                vmem((3, 8, 8, 128), F32),
                vmem((4, 4, 8, 128), F32),
                vmem((3, 8, 8, 128), F32),
                vmem((zs * xs, 1, 128), F32),
                dma((12,)),
                dma((2,)),
                dma((2,)),
                dma((2,)),
                dma((2,)),
                dma((2, 4, 7)),
                dma((2, 4, 2, 8)),
                dma((3,)),
                dma((3,)),
                dma((2,)),
                dma((2,)),
                dma((2,)),
                dma((2,)),
                dma((2,)),
                pltpu.SemaphoreType.REGULAR((4,)),
            ],
            compiler_params=pltpu.CompilerParams(
                collective_id=0, has_side_effects=True, vmem_limit_bytes=VLIM * 1024 * 1024
            ),
        )(
            pops, kinetic.T, sto, draws, rates, adjacency.T, tallies.transpose(0, 2, 1), coef,
            target, msf, prior,
        )

    return jax.shard_map(
        shards,
        mesh=mesh,
        in_specs=(
            P("narrow", "wide", None),
            P(),
            P(),
            P(None, None, ("wide", "narrow"), None),
            P("narrow"),
            P("wide", None),
            P(None, "wide", None),
            P("narrow"),
            P("wide", None),
            P("wide", "narrow"),
            P("wide", "narrow"),
        ),
        out_specs=(P("narrow", "wide", None), P("wide", "narrow")),
        check_vma=False,
    )
```
